128 devices in a mesh: blk: 8 (over y_lo, x), hid: 16 (over y_hi, z, core).
Axes of the slice: x: 4, y: 4 (y_hi: 2, y_lo: 2; y = y_hi * 2 + y_lo), z: 4, core: 2. Of those that a mesh axis runs over, the one named last changes fastest.
Arguments:
- images: bfloat16 [32768, 1024], P(('blk', 'hid')), may hold values from -0.1875 to 0.1875
- caption_ids: int32 [32768], P(('blk', 'hid')), may hold values from 0 to 8191, as said below
- captions: bfloat16 [8192, 1024], P(('blk', 'hid')), may hold values from -0.75 to 0.75
- caption_feats: bfloat16 [8192, 1024], P(('blk', 'hid')), may hold values from -1.5 to 1.5
- w_in: bfloat16 [1024, 32768], P('blk', 'hid'), may hold values from -0.1875 to 0.1875
- w_out: bfloat16 [1024, 32768], P('blk', 'hid'), may hold values from -0.03125 to 0.03125
- logit_scale: float32 [1], replicated, may hold values from 8 to 16
- logit_bias: float32 [1], replicated, may hold values from -3 to -1
Outputs:
- image_grad: bfloat16 [32768, 1024], P(('blk', 'hid'))
- feat_grad: bfloat16 [8192, 1024], P(('blk', 'hid'))
- w_in_grad: bfloat16 [1024, 32768], P('blk', 'hid')
- w_out_grad: bfloat16 [1024, 32768], P('blk', 'hid')
The draws below stay inside these ranges and needn't reach their ends.
Inputs may be any that keep to these rules, and one draw needn't show every extreme that they name: `caption_ids`: the image rows of block b name caption rows of the caption blocks b, b - 1, ..., b - 2 (mod the number of blocks); the first image row of every block names the last caption row of its own block, the second names the first.
All inputs are finite; a program needn't handle non-finite values.
Results may differ from the reference program's by a relative error of at most 0.019.
Values may be sent and summed in bfloat16 or wider, within the bound.
No kernel may reach another device: no remote copies, remote signals or barrier semaphores. Data moves between devices by JAX's collectives and lax.ppermute only.
A program may use at most 128 MiB of HBM per device.

```python
import math
import jax
import jax.numpy as jnp
from jax import lax

D = 1024
FF = 32768
IMG_DEV = 256
CAP_DEV = 64
HOPS = 2
IMAGES = 32768
CAPTIONS = 8192
GROUP_ROWS = 1024
N_BLK = 8
N_HID = 16


def draw_caption_ids(key, part):
    devices = N_BLK * N_HID
    key_hop, key_row = jax.random.split(jax.random.fold_in(key, 17))
    hops = jax.random.randint(key_hop, (devices, IMG_DEV), 0, HOPS + 1, dtype=jnp.int32)
    rows = jax.random.randint(key_row, (devices, IMG_DEV), 0, CAP_DEV, dtype=jnp.int32)
    column = jnp.arange(IMG_DEV, dtype=jnp.int32)[None, :]
    hops = jnp.where(column < 2, 0, hops)
    rows = jnp.where(column == 0, CAP_DEV - 1, jnp.where(column == 1, 0, rows))
    blocks = (jnp.arange(devices, dtype=jnp.int32)[:, None] - hops) % devices
    return (blocks * CAP_DEV + rows).reshape(-1).astype(jnp.int32)


def block_scale(own_key, dims, shards, low, top_value):
    gain = 1.0
    for dim, shards_of in shards:
        heights = jax.random.uniform(jax.random.fold_in(jax.random.fold_in(own_key, 6), dim), (shards_of,), jnp.float32, low / len(shards), top_value / len(shards))
        gain = gain * jnp.repeat(jnp.exp(heights), dims[dim] // shards_of).reshape((-1,) + (1,) * (len(dims) - 1 - dim))
    return gain


def bell_draw(stream_key, dims, deviation, limit, cuts=(), kind=jnp.bfloat16):
    drawn = jax.random.normal(stream_key, dims, jnp.float32) * deviation
    if len(cuts) > 0:
        drawn = block_scale(stream_key, dims, cuts, -0.22, 0.18) * drawn
    return jnp.clip(drawn, min=-limit, max=limit).astype(kind)


def setup_inputs(seed: int = 0) -> dict:
    streams_of = jax.random.split(jax.random.key(seed), 9)
    images = bell_draw(streams_of[0], (IMAGES, D), 0.03, 0.1875, ((0, 128),))
    caption_ids = draw_caption_ids(jax.random.fold_in(streams_of[8], 71), 0)
    captions = bell_draw(streams_of[2], (CAPTIONS, D), 0.125, 0.75, ((0, 128),))
    caption_feats = bell_draw(streams_of[3], (CAPTIONS, D), 0.25, 1.5, ((0, 128),))
    w_in = bell_draw(streams_of[4], (D, FF), D ** -0.5, 0.1875, ((0, 8), (1, 16)))
    w_out = bell_draw(streams_of[5], (D, FF), FF ** -0.5, 0.03125, ((0, 8), (1, 16)))
    logit_scale = jnp.clip(jnp.exp(jax.random.uniform(streams_of[6], (1,), jnp.float32, math.log(8.0), math.log(16.0))), 8.0, 16.0)
    logit_bias = jnp.clip(jax.random.uniform(streams_of[7], (1,), jnp.float32, -3.0, -1.0), -3.0, -1.0)
    return {"images": images, "caption_ids": caption_ids, "captions": captions, "caption_feats": caption_feats, "w_in": w_in, "w_out": w_out, "logit_scale": logit_scale, "logit_bias": logit_bias}


def gelu_parts(values):
    coefficient = math.sqrt(2.0 / math.pi)
    inner_arg = coefficient * (values + 0.044715 * values * values * values)
    tangent = jnp.tanh(inner_arg)
    output = 0.5 * values * (1.0 + tangent)
    gelu_slope = 0.5 * (1.0 + tangent) + 0.5 * values * (1.0 - tangent * tangent) * coefficient * (1.0 + 3.0 * 0.044715 * values * values)
    return (output, gelu_slope)

def contract(left_side, right_side, left_dim, right_dim):
    return lax.dot_general(left_side, right_side, (((left_dim,), (right_dim,)), ((), ())), preferred_element_type=jnp.float32)

def reference(images, caption_ids, captions, caption_feats, w_in, w_out, logit_scale, logit_bias):
    devices = N_BLK * N_HID
    temper = logit_scale[0]
    offset = logit_bias[0]
    image_blocks = images.reshape(devices, IMG_DEV, D)
    id_blocks = caption_ids.reshape(devices, IMG_DEV)
    cap_blocks = captions.reshape(devices, CAP_DEV, D)
    owners = jnp.arange(devices, dtype=jnp.int32)
    cap_local = jnp.arange(CAP_DEV, dtype=jnp.int32)

    def one_device(inputs):
        image_rows, id_rows, device = inputs
        image_acc = jnp.zeros((IMG_DEV, D), jnp.float32)
        hop_terms = []
        for stride in range(HOPS + 1):
            holder = ((device - stride) % devices).astype(jnp.int32)
            current = lax.dynamic_index_in_dim(cap_blocks, holder, 0, keepdims=False)
            logits = temper * contract(current, image_rows, 1, 1) + offset
            global_rows = holder * CAP_DEV + cap_local
            positive = (global_rows[:, None] == id_rows[None, :]).astype(jnp.float32)
            pair_grad = (jax.nn.sigmoid(logits) - positive).astype(jnp.bfloat16)
            image_acc = image_acc + contract(pair_grad, current, 0, 0)
            hop_terms.append(temper * jnp.dot(pair_grad, image_rows, preferred_element_type=jnp.float32))
        return ((temper * image_acc).astype(jnp.bfloat16), jnp.stack(hop_terms))
    image_out, term_blocks = lax.map(one_device, (image_blocks, id_blocks, owners))
    cap_acc = term_blocks[:, 0]
    for stride in range(1, HOPS + 1):
        cap_acc = cap_acc + jnp.roll(term_blocks[:, stride], -stride, axis=0)
    caption_grad = cap_acc.reshape(CAPTIONS, D)
    caption_round = caption_grad.astype(jnp.bfloat16)
    grad_groups = caption_round.reshape(N_BLK, GROUP_ROWS, D)
    feat_groups = caption_feats.reshape(N_BLK, GROUP_ROWS, D)

    def group_step(totals, pair):
        grad_rows, feat_rows = pair
        pre_act = jnp.dot(feat_rows, w_in, preferred_element_type=jnp.float32)
        act_grad = jnp.dot(grad_rows, w_out, preferred_element_type=jnp.float32)
        output, gelu_slope = gelu_parts(pre_act)
        active = output.astype(jnp.bfloat16)
        pre_grad = (act_grad * gelu_slope).astype(jnp.bfloat16)
        in_part = lax.optimization_barrier(contract(feat_rows, pre_grad, 0, 0).astype(jnp.bfloat16)).astype(jnp.float32)
        out_part = lax.optimization_barrier(contract(grad_rows, active, 0, 0).astype(jnp.bfloat16)).astype(jnp.float32)
        branch = contract(pre_grad, w_in, 1, 1)
        return ((totals[0] + in_part, totals[1] + out_part), branch)
    zero_init = jnp.zeros((D, FF), jnp.float32)
    sums, branches = lax.scan(group_step, (zero_init, zero_init), (grad_groups, feat_groups))
    feat_grad = (caption_grad + branches.reshape(CAPTIONS, D)).astype(jnp.bfloat16)
    return (image_out.reshape(IMAGES, D), feat_grad, sums[0].astype(jnp.bfloat16), sums[1].astype(jnp.bfloat16))
```

```python
import math

import jax
import jax.numpy as jnp
from jax import lax
from jax.sharding import Mesh
from jax.sharding import PartitionSpec as P

HOPS = 2
AXES = ("yl", "x", "yh", "z", "c")
Y = ("yl", "yh")
BF = jnp.bfloat16
F32 = jnp.float32


def from_behind(shard, axis, by):
    length = lax.axis_size(axis)
    if axis == Y:
        place = [(y % 2) * 2 + y // 2 for y in range(4)]
    else:
        place = list(range(length))
    pairs = [(place[i], place[(i + by) % length]) for i in range(length)]
    return lax.ppermute(shard, axis, pairs)


def gelu_parts(values):
    coefficient = math.sqrt(2.0 / math.pi)
    inner_arg = coefficient * (values + 0.044715 * values * values * values)
    tangent = jnp.tanh(inner_arg)
    output = 0.5 * values * (1.0 + tangent)
    gelu_slope = 0.5 * (1.0 + tangent) + 0.5 * values * (1.0 - tangent * tangent) * coefficient * (
        1.0 + 3.0 * 0.044715 * values * values
    )
    return (output, gelu_slope)


def contract(left_side, right_side, left_dim, right_dim):
    return lax.dot_general(
        left_side,
        right_side,
        (((left_dim,), (right_dim,)), ((), ())),
        preferred_element_type=F32,
    )


def to_order(rows):
    n = rows.shape[0]
    return rows.reshape(n, 2, 4, 128).transpose(0, 2, 1, 3).reshape(n, 1024)


def from_order(rows):
    n = rows.shape[0]
    return rows.reshape(n, 4, 2, 128).transpose(0, 2, 1, 3).reshape(n, 1024)


def gather_axis(block, axis):
    n = lax.axis_size(axis)
    return jnp.concatenate([block] + [from_behind(block, axis, k) for k in range(1, n)], axis=0)


def gather_rows(block):
    return gather_axis(gather_axis(gather_axis(block, "z"), Y), "c")


def scatter_axis(block, axis):
    n = lax.axis_size(axis)
    parts = block.reshape(n, block.shape[0] // n, block.shape[1])
    total = parts[0]
    for k in range(1, n):
        total = total + from_behind(parts[k].astype(BF), axis, -k).astype(F32)
    return total


def scatter_rows(block):
    return scatter_axis(scatter_axis(scatter_axis(block, "c"), Y), "z")


def weight_full(shard):
    halves = shard.reshape(128, 2, 1024).transpose(1, 0, 2)
    sent = jnp.broadcast_to(halves[None], (4, 2, 128, 1024)).reshape(1024, 1024)
    return lax.all_to_all(sent, ("x", "yl"), 0, 0, tiled=True)


def grad_shard(partial):
    got = lax.all_to_all(partial.astype(BF), ("x", "yl"), 0, 0, tiled=True)
    total = got.reshape(4, 2, 128, 1024).astype(F32).sum(0)
    return total.transpose(1, 0, 2).reshape(128, 2048).astype(BF)


def shards(images, caption_ids, captions, caption_feats, w_in, w_out, logit_scale, logit_bias):
    temper = logit_scale[0]
    offset = logit_bias[0]
    cap_rows = captions.shape[0]
    devices = lax.axis_size(AXES)
    device = lax.axis_index(AXES)
    cap_local = lax.broadcasted_iota(jnp.int32, (cap_rows, 1), 0)

    blocks = [captions] + [from_behind(captions, AXES, k) for k in range(1, HOPS + 1)]
    full_in = weight_full(w_in)
    full_out = weight_full(w_out)
    feats_all = gather_rows(to_order(caption_feats))

    current = jnp.concatenate(blocks, axis=0)
    rows = jnp.concatenate(
        [((device - k) % devices) * cap_rows + cap_local for k in range(HOPS + 1)], axis=0
    )
    positive = (rows == caption_ids[None, :]).astype(F32)
    logits = temper * contract(current, images, 1, 1) + offset
    pair_grad = (jax.nn.sigmoid(logits) - positive).astype(BF)
    terms = temper * contract(pair_grad, images, 1, 0)
    image_grad = (temper * contract(pair_grad, current, 0, 0)).astype(BF)
    own_grad = terms[:cap_rows]
    for k in range(1, HOPS + 1):
        part = terms[k * cap_rows : (k + 1) * cap_rows].astype(BF)
        own_grad = own_grad + from_behind(part, AXES, -k).astype(F32)
    caption_round = own_grad.astype(BF)
    rows_all = gather_rows(to_order(caption_round))

    pre_act = contract(feats_all, full_in, 1, 0)
    output, gelu_slope = gelu_parts(pre_act)
    active = output.astype(BF)
    w_out_grad = grad_shard(contract(rows_all, active, 0, 0))
    act_grad = contract(rows_all, full_out, 1, 0)
    pre_grad = (act_grad * gelu_slope).astype(BF)
    w_in_grad = grad_shard(contract(feats_all, pre_grad, 0, 0))
    branch = from_order(scatter_rows(contract(pre_grad, full_in, 1, 1)))
    feat_grad = (own_grad + branch).astype(BF)
    return (image_grad, feat_grad, w_in_grad, w_out_grad)


def solution(mesh):
    fine = Mesh(mesh.devices.reshape(2, 4, 2, 4, 2), AXES)
    rows = P(AXES, None)
    weights = P(("yl", "x"), ("yh", "z", "c"))
    return jax.shard_map(
        shards,
        mesh=fine,
        in_specs=(rows, P(AXES), rows, rows, weights, weights, P(), P()),
        out_specs=(rows, rows, weights, weights),
        check_vma=False,
    )
```

```python
import math

import jax
import jax.numpy as jnp
from jax import lax
from jax.experimental import pallas as pl
from jax.experimental.pallas import tpu as pltpu
from jax.sharding import Mesh
from jax.sharding import PartitionSpec as P

HOPS = 2
AXES = ("yl", "x", "yh", "z", "c")
BF = jnp.bfloat16
F32 = jnp.float32


def from_behind(shard, axis, by):
    length = lax.axis_size(axis)
    return lax.ppermute(shard, axis, [(i, (i + by) % length) for i in range(length)])


def step_pairs(first, by):
    pairs = []
    for yl in range(2):
        for yh in range(2):
            for z in range(4):
                for c in range(2):
                    if (c == 0) == first:
                        to = (yl, yh, (z + by) % 4, c)
                    else:
                        y = (yh * 2 + yl + by) % 4
                        to = (y % 2, y // 2, z, c)
                    pairs.append((flat(yl, yh, z, c), flat(*to)))
    return pairs


def flat(yl, yh, z, c):
    return ((yl * 2 + yh) * 4 + z) * 2 + c


def step(shard, first, by):
    return lax.ppermute(shard, ("yl", "yh", "z", "c"), step_pairs(first, by))


def swap_core(shard):
    return lax.ppermute(shard, "c", [(0, 1), (1, 0)])


def pack(pieces):
    rows, width = pieces[0].shape
    count = len(pieces)

    def kernel(*refs):
        out, sem = refs[count], refs[count + 1]
        copies = [
            pltpu.make_async_copy(refs[i], out.at[pl.ds(i * rows, rows)], sem.at[i])
            for i in range(count)
        ]
        for copy in copies:
            copy.start()
        for copy in copies:
            copy.wait()

    return pl.pallas_call(
        kernel,
        out_shape=jax.ShapeDtypeStruct((rows * count, width), pieces[0].dtype),
        in_specs=[pl.BlockSpec(memory_space=pl.ANY)] * count,
        out_specs=pl.BlockSpec(memory_space=pl.ANY),
        scratch_shapes=[pltpu.SemaphoreType.DMA((count,))],
    )(*pieces)


def gelu_parts(values):
    coefficient = math.sqrt(2.0 / math.pi)
    inner_arg = coefficient * (values + 0.044715 * values * values * values)
    tangent = jnp.tanh(inner_arg)
    output = 0.5 * values * (1.0 + tangent)
    gelu_slope = 0.5 * (1.0 + tangent) + 0.5 * values * (1.0 - tangent * tangent) * coefficient * (
        1.0 + 3.0 * 0.044715 * values * values
    )
    return (output, gelu_slope)


def contract(left_side, right_side, left_dim, right_dim):
    return lax.dot_general(
        left_side,
        right_side,
        (((left_dim,), (right_dim,)), ((), ())),
        preferred_element_type=F32,
    )


def gather_rows(block):
    for_next = pack([block] + [step(block, True, k) for k in range(1, 4)])
    own = [for_next] + [step(for_next, False, k) for k in range(1, 4)]
    return pack(own + [swap_core(piece) for piece in own]), for_next


def scatter_rows(own, other):
    total = own.astype(F32) + swap_core(other).astype(F32)
    for first in (False, True):
        parts = total.reshape(4, total.shape[0] // 4, total.shape[1])
        sent = parts.astype(BF)
        total = parts[0]
        for k in range(1, 4):
            total = total + step(sent[k], first, -k).astype(F32)
    return total


def call(kernel, grid, ins, outs, *args, after=(), flops=0):
    taken = len(args)

    def body(*refs):
        kernel(*refs[:taken], *refs[taken + len(after) :])

    return pl.pallas_call(
        body,
        grid=grid,
        in_specs=ins + [pl.BlockSpec(memory_space=pl.ANY)] * len(after),
        out_specs=[spec for spec, _ in outs],
        out_shape=[shape for _, shape in outs],
        compiler_params=pltpu.CompilerParams(vmem_limit_bytes=28 << 20),
        cost_estimate=pl.CostEstimate(
            flops=flops,
            bytes_accessed=sum(a.size * a.dtype.itemsize for a in args)
            + sum(shape.size * shape.dtype.itemsize for _, shape in outs),
            transcendentals=0,
        ),
    )(*args, *after)


def add_hops(parts, after):
    rows, width = parts[0].shape

    def kernel(a, b, c, total, rounded):
        value = a[...] + b[...].astype(F32) + c[...].astype(F32)
        total[...] = value
        rounded[...] = value.astype(BF)

    whole = pl.BlockSpec((rows, width), lambda: (0, 0))
    return call(
        kernel,
        (),
        [whole] * 3,
        [(whole, jax.ShapeDtypeStruct((rows, width), kind)) for kind in (F32, BF)],
        *parts,
        after=after,
    )


def forward_layer(feats, full):
    n, d = feats.shape
    m = full.shape[1]
    tn, tm = 512, 512

    def kernel(a, b, active, slope):
        output, gelu_slope = gelu_parts(contract(a[...], b[...], 1, 0))
        active[...] = output.astype(BF)
        slope[...] = gelu_slope.astype(BF)

    tile = pl.BlockSpec((tn, tm), lambda j, i: (i, j))
    return call(
        kernel,
        (m // tm, n // tn),
        [pl.BlockSpec((tn, d), lambda j, i: (i, 0)), pl.BlockSpec((d, tm), lambda j, i: (0, j))],
        [(tile, jax.ShapeDtypeStruct((n, m), BF))] * 2,
        feats,
        full,
        flops=2 * n * d * m,
    )


def backward_act(rows, full, slope, after):
    n, d = rows.shape
    m = full.shape[1]
    tn, tm = 512, 512

    def kernel(a, b, s, out):
        out[...] = (contract(a[...], b[...], 1, 0) * s[...].astype(F32)).astype(BF)

    tile = pl.BlockSpec((tn, tm), lambda j, i: (i, j))
    return call(
        kernel,
        (m // tm, n // tn),
        [
            pl.BlockSpec((tn, d), lambda j, i: (i, 0)),
            pl.BlockSpec((d, tm), lambda j, i: (0, j)),
            tile,
        ],
        [(tile, jax.ShapeDtypeStruct((n, m), BF))],
        rows,
        full,
        slope,
        after=after,
        flops=2 * n * d * m,
    )[0]


def product(a, b, left_dim, right_dim, start=0, n=None, after=()):
    k = a.shape[left_dim]
    n = a.shape[1 - left_dim] if n is None else n
    m = b.shape[1 - right_dim]
    tn, tm = 512, 512
    first = start // tn

    def kernel(left, right, out):
        out[...] = contract(left[...], right[...], left_dim, right_dim).astype(BF)

    left = (
        pl.BlockSpec((tn, k), lambda j, i: (first + i, 0))
        if left_dim == 1
        else pl.BlockSpec((k, tn), lambda j, i: (0, first + i))
    )
    right = (
        pl.BlockSpec((tm, k), lambda j, i: (j, 0))
        if right_dim == 1
        else pl.BlockSpec((k, tm), lambda j, i: (0, j))
    )
    return call(
        kernel,
        (m // tm, n // tn),
        [left, right],
        [(pl.BlockSpec((tn, tm), lambda j, i: (i, j)), jax.ShapeDtypeStruct((n, m), BF))],
        a,
        b,
        after=after,
        flops=2 * n * m * k,
    )[0]


def spread(shard, after=()):
    n, m = shard.shape
    half = m // 2

    def kernel(*refs):
        source, out, sem = refs[0], refs[-2], refs[-1]
        copies = [
            pltpu.make_async_copy(
                source.at[:, pl.ds(yl * half, half)], out.at[yl * 4 + x], sem.at[yl * 4 + x]
            )
            for yl in range(2)
            for x in range(4)
        ]
        for copy in copies:
            copy.start()
        for copy in copies:
            copy.wait()

    return pl.pallas_call(
        kernel,
        out_shape=jax.ShapeDtypeStruct((8, n, half), shard.dtype),
        in_specs=[pl.BlockSpec(memory_space=pl.ANY)] * (1 + len(after)),
        out_specs=pl.BlockSpec(memory_space=pl.ANY),
        scratch_shapes=[pltpu.SemaphoreType.DMA((8,))],
    )(shard, *after)


def weight_full(shard, after=()):
    got = lax.all_to_all(spread(shard, after), ("yl", "x"), 0, 0, tiled=True)
    return got.reshape(1024, 1024)


def grad_shard(partial):
    got = lax.all_to_all(partial, ("yl", "x"), 0, 0, tiled=True).reshape(2, 4, 128, 1024)

    def kernel(parts, out):
        out[...] = parts[0].astype(F32).sum(0).astype(BF)

    return call(
        kernel,
        (2,),
        [pl.BlockSpec((1, 4, 128, 1024), lambda j: (j, 0, 0, 0))],
        [(pl.BlockSpec((128, 1024), lambda j: (0, j)), jax.ShapeDtypeStruct((128, 2048), BF))],
        got,
    )[0]


def shards(images, caption_ids, captions, caption_feats, w_in, w_out, logit_scale, logit_bias):
    temper = logit_scale[0]
    offset = logit_bias[0]
    cap_rows = captions.shape[0]
    devices = lax.axis_size(AXES)
    device = lax.axis_index(AXES)
    cap_local = lax.broadcasted_iota(jnp.int32, (cap_rows, 1), 0)

    blocks = [captions] + [from_behind(captions, AXES, k) for k in range(1, HOPS + 1)]
    full_in = weight_full(w_in)
    feats_all, feats_part = gather_rows(caption_feats)

    current = jnp.concatenate(blocks, axis=0)
    rows = jnp.concatenate(
        [((device - k) % devices) * cap_rows + cap_local for k in range(HOPS + 1)], axis=0
    )
    positive = (rows == caption_ids[None, :]).astype(F32)
    logits = temper * contract(current, images, 1, 1) + offset
    pair_grad = (jax.nn.sigmoid(logits) - positive).astype(BF)
    terms = temper * contract(pair_grad, images, 1, 0)
    image_grad = (temper * contract(pair_grad, current, 0, 0)).astype(BF)
    parts = [terms[:cap_rows]]
    for k in range(1, HOPS + 1):
        part = terms[k * cap_rows : (k + 1) * cap_rows].astype(BF)
        parts.append(from_behind(part, AXES, -k))
    own_grad, caption_round = add_hops(parts, (feats_part,))
    rows_all, rows_part = gather_rows(caption_round)
    full_out = weight_full(w_out, (rows_part,))

    active, slope = forward_layer(feats_all, full_in)
    out_part = product(rows_all, active, 0, 0)
    w_out_grad = grad_shard(out_part)
    pre_grad = backward_act(rows_all, full_out, slope, (out_part,))
    in_part = product(feats_all, pre_grad, 0, 0)
    w_in_grad = grad_shard(in_part)
    half = rows_all.shape[0] // 2
    other = product(pre_grad, full_in, 1, 1, half, half, (in_part,))
    own = product(pre_grad, full_in, 1, 1, 0, half)
    branch = scatter_rows(own, other)
    feat_grad = (own_grad + branch).astype(BF)
    return (image_grad, feat_grad, w_in_grad, w_out_grad)


def solution(mesh):
    fine = Mesh(mesh.devices.reshape(2, 4, 2, 4, 2), AXES)
    rows = P(AXES, None)
    weights = P(("yl", "x"), ("yh", "z", "c"))
    return jax.shard_map(
        shards,
        mesh=fine,
        in_specs=(rows, P(AXES), rows, rows, weights, weights, P(), P()),
        out_specs=(rows, rows, weights, weights),
        check_vma=False,
    )
```

```python
import math

import jax
import jax.numpy as jnp
from jax import lax
from jax.experimental import pallas as pl
from jax.experimental.pallas import tpu as pltpu
from jax.sharding import Mesh
from jax.sharding import PartitionSpec as P

HOPS = 2
AXES = ("yl", "x", "yh", "z", "c")
BF = jnp.bfloat16
F32 = jnp.float32


def from_behind(shard, axis, by):
    length = lax.axis_size(axis)
    return lax.ppermute(shard, axis, [(i, (i + by) % length) for i in range(length)])


def step_pairs(first, by):
    pairs = []
    for yl in range(2):
        for yh in range(2):
            for z in range(4):
                for c in range(2):
                    if (c == 0) == first:
                        to = (yl, yh, (z + by) % 4, c)
                    else:
                        y = (yh * 2 + yl + by) % 4
                        to = (y % 2, y // 2, z, c)
                    pairs.append((flat(yl, yh, z, c), flat(*to)))
    return pairs


def flat(yl, yh, z, c):
    return ((yl * 2 + yh) * 4 + z) * 2 + c


def step(shard, first, by):
    return lax.ppermute(shard, ("yl", "yh", "z", "c"), step_pairs(first, by))


def swap_core(shard):
    return lax.ppermute(shard, "c", [(0, 1), (1, 0)])


def pack(pieces, after=()):
    rows, width = pieces[0].shape
    count = len(pieces)

    def kernel(*refs):
        out, sem = refs[-2], refs[-1]
        copies = [
            pltpu.make_async_copy(refs[i], out.at[pl.ds(i * rows, rows)], sem.at[i])
            for i in range(count)
        ]
        for copy in copies:
            copy.start()
        for copy in copies:
            copy.wait()

    return pl.pallas_call(
        kernel,
        out_shape=jax.ShapeDtypeStruct((rows * count, width), pieces[0].dtype),
        in_specs=[pl.BlockSpec(memory_space=pl.ANY)] * (count + len(after)),
        out_specs=pl.BlockSpec(memory_space=pltpu.VMEM),
        scratch_shapes=[pltpu.SemaphoreType.DMA((count,))],
        compiler_params=pltpu.CompilerParams(vmem_limit_bytes=16 << 20),
    )(*pieces, *after)


def gelu_parts(values):
    coefficient = math.sqrt(2.0 / math.pi)
    square = values * values
    tangent = jnp.tanh(values * (coefficient + coefficient * 0.044715 * square))
    share = 0.5 + 0.5 * tangent
    output = values * share
    gelu_slope = share + output * (1.0 - share) * (
        2.0 * coefficient + 6.0 * coefficient * 0.044715 * square
    )
    return (output, gelu_slope)


def contract(left_side, right_side, left_dim, right_dim):
    return lax.dot_general(
        left_side,
        right_side,
        (((left_dim,), (right_dim,)), ((), ())),
        preferred_element_type=F32,
    )


def gather_first(block, after=()):
    return pack([block] + [step(block, True, k) for k in range(1, 4)], after)


def gather_second(block):
    own = [block] + [step(block, False, k) for k in range(1, 4)]
    return own, [swap_core(piece) for piece in own]


def add_split(arrays):
    n, width = arrays[0].shape
    rows = n // 4
    count = len(arrays)

    def kernel(*refs):
        for k in range(4):
            at = pl.ds(k * rows, rows)
            total = refs[0][at, :].astype(F32)
            for a in refs[1:count]:
                total = total + a[at, :].astype(F32)
            refs[count + k][...] = total.astype(refs[count + k].dtype)

    vmem = pl.BlockSpec(memory_space=pltpu.VMEM)
    return pl.pallas_call(
        kernel,
        out_shape=[jax.ShapeDtypeStruct((rows, width), kind) for kind in (F32, BF, BF, BF)],
        in_specs=[vmem] * count,
        out_specs=[vmem] * 4,
        compiler_params=pltpu.CompilerParams(vmem_limit_bytes=20 << 20),
    )(*arrays)


def scatter_rows(own, other, own_grad):
    arrays = [own, swap_core(other)]
    for first in (False, True):
        parts = add_split(arrays)
        arrays = [parts[0]] + [step(parts[k], first, -k) for k in range(1, 4)]
    return add_branch(arrays[0], arrays[1:], own_grad)


def add_branch(own, received, own_grad):
    rows, width = own.shape

    def kernel(a, b, c, d, grad, out):
        value = a[...] + b[...].astype(F32) + c[...].astype(F32) + d[...].astype(F32)
        out[...] = (grad[...] + value).astype(BF)

    whole = pl.BlockSpec((rows, width), lambda: (0, 0))
    return call(
        kernel,
        (),
        [whole] * 5,
        [(whole, jax.ShapeDtypeStruct((rows, width), BF))],
        own,
        *received,
        own_grad,
    )[0]


def call(kernel, grid, ins, outs, *args, after=(), flops=0):
    taken = len(args)

    def body(*refs):
        kernel(*refs[:taken], *refs[taken + len(after) :])

    return pl.pallas_call(
        body,
        grid=grid,
        in_specs=ins + [pl.BlockSpec(memory_space=pl.ANY)] * len(after),
        out_specs=[spec for spec, _ in outs],
        out_shape=[shape for _, shape in outs],
        compiler_params=pltpu.CompilerParams(vmem_limit_bytes=20 << 20),
        cost_estimate=pl.CostEstimate(
            flops=flops,
            bytes_accessed=sum(a.size * a.dtype.itemsize for a in args)
            + sum(shape.size * shape.dtype.itemsize for _, shape in outs),
            transcendentals=0,
        ),
    )(*args, *after)


def add_hops(parts, after):
    rows, width = parts[0].shape

    def kernel(a, b, c, total, rounded):
        value = a[...] + b[...].astype(F32) + c[...].astype(F32)
        total[...] = value
        rounded[...] = value.astype(BF)

    whole = pl.BlockSpec((rows, width), lambda: (0, 0))
    return call(
        kernel,
        (),
        [whole] * 3,
        [(whole, jax.ShapeDtypeStruct((rows, width), kind)) for kind in (F32, BF)],
        *parts,
        after=after,
    )


def local_copies(plan, out, count, *args, vmem=16):
    def kernel(*refs):
        target, sem = refs[-2], refs[-1]
        copies = [
            pltpu.make_async_copy(a, b, sem.at[i])
            for i, (a, b) in enumerate(plan(refs[:-2], target))
        ]
        for copy in copies:
            copy.start()
        for copy in copies:
            copy.wait()

    return pl.pallas_call(
        kernel,
        out_shape=jax.ShapeDtypeStruct(out, BF),
        in_specs=[
            pl.BlockSpec(memory_space=pltpu.SMEM if a.dtype == jnp.int32 else pl.ANY) for a in args
        ],
        out_specs=pl.BlockSpec(memory_space=pltpu.VMEM),
        scratch_shapes=[pltpu.SemaphoreType.DMA((count,))],
        compiler_params=pltpu.CompilerParams(vmem_limit_bytes=vmem << 20),
    )(*args)


def spread(parts, after=()):
    n, m = parts[0].shape
    count = len(parts)

    def plan(refs, out):
        return [(refs[k], out.at[x, k]) for x in range(4) for k in range(count)]

    sent = local_copies(plan, (4, count, n, m), 4 * count, *parts, *after)
    return lax.all_to_all(sent, "x", 0, 0, tiled=True)


def behind(array, after):
    def kernel(a, b, out):
        pass

    anywhere = pl.BlockSpec(memory_space=pl.ANY)
    return pl.pallas_call(
        kernel,
        out_shape=jax.ShapeDtypeStruct(array.shape, array.dtype),
        in_specs=[anywhere] * 2,
        out_specs=anywhere,
        input_output_aliases={0: 0},
    )(array, after)


def kernel_of(body, outs, scratch, copies, flops, place, *arrays):
    vmem = [pltpu.VMEM(shape, BF) for shape in scratch]
    return pl.pallas_call(
        body,
        out_shape=[jax.ShapeDtypeStruct(shape, BF) for shape in outs],
        in_specs=[pl.BlockSpec(memory_space=pltpu.SMEM)]
        + [pl.BlockSpec(memory_space=pl.ANY)] * len(arrays),
        out_specs=[pl.BlockSpec(memory_space=pl.ANY)] * len(outs),
        scratch_shapes=vmem + [pltpu.SemaphoreType.DMA((copies,))],
        compiler_params=pltpu.CompilerParams(vmem_limit_bytes=60 << 20),
        cost_estimate=pl.CostEstimate(
            flops=flops,
            bytes_accessed=2 * sum(a.size for a in arrays) + 2 * sum(math.prod(o) for o in outs),
            transcendentals=0,
        ),
    )(place, *arrays)


class Copies:
    def __init__(self, sem):
        self.sem, self.count = sem, 0

    def start(self, source, target):
        copy = pltpu.make_async_copy(source, target, self.sem.at[self.count])
        self.count += 1
        copy.start()
        return copy


def load_rows(copies, pieces, target):
    n = pieces[0].shape[0]
    return [
        copies.start(piece, target.at[pl.ds(i * n, n)]) for i, piece in enumerate(pieces)
    ]


def load_weight(copies, got, target, yl):
    return [
        copies.start(
            got.at[x, k],
            target.at[pl.ds(pl.multiple_of(lax.rem(yl + k, 2) * 512 + x * 128, 128), 128)],
        )
        for k in range(2)
        for x in range(4)
    ]


def wait(copies):
    for copy in copies:
        copy.wait()


CHUNK = 512
BLOCK = 256


def forward(place, feats, got_in, rows):
    n, d, m = 8 * feats[0].shape[0], feats[0].shape[1], got_in.shape[-1]

    def body(*refs):
        yl = refs[0][0]
        feat_refs, w_ref, row_refs = refs[1:9], refs[9], refs[10:18]
        slope_out, grad_out = refs[18:20]
        f, w, r, active, slope, grad, sem = refs[20:]
        copies = Copies(sem)
        w_copies = load_weight(copies, w_ref, w, yl)
        f_copies = load_rows(copies, feat_refs, f)
        r_copies = load_rows(copies, row_refs, r)
        last = []
        wait(w_copies)
        for i in range(n // CHUNK):
            wait(f_copies[2 * i : 2 * i + 2])
            at = pl.ds(i * CHUNK, CHUNK)
            output, gelu_slope = gelu_parts(contract(f[at, :], w[...], 1, 0))
            active[at, :] = output.astype(BF)
            slope[at, :] = gelu_slope.astype(BF)
            last.append(copies.start(slope.at[at], slope_out.at[at]))
        wait(r_copies)
        for j in range(d // BLOCK):
            at = pl.ds(j * BLOCK, BLOCK)
            grad[at, :] = contract(r[:, j * BLOCK : (j + 1) * BLOCK], active[...], 0, 0).astype(BF)
            last.append(copies.start(grad.at[at], grad_out.at[at]))
        wait(last)

    return kernel_of(
        body,
        [(n, m), (d, m)],
        [(n, d), (d, m), (n, d), (n, m), (n, m), (d, m)],
        32,
        4 * n * d * m,
        place,
        *feats,
        got_in,
        *rows,
    )


def backward(place, rows, got_out, slope, got_in, feats):
    n, d, m = 8 * feats[0].shape[0], feats[0].shape[1], got_in.shape[-1]
    half = n // 2

    def body(*refs):
        yl = refs[0][0]
        row_refs, w_out_ref, slope_ref, w_in_ref, feat_refs = (
            refs[1:9],
            refs[9],
            refs[10],
            refs[11],
            refs[12:20],
        )
        other_out, own_out, grad_out = refs[20:23]
        r, w_out, slope, w_in, f, pre, branch, grad, sem = refs[23:]
        copies = Copies(sem)
        order = [2, 3, 0, 1]
        w_copies = load_weight(copies, w_out_ref, w_out, yl)
        r_copies = load_rows(copies, row_refs, r)
        s_copies = [
            copies.start(slope_ref.at[pl.ds(i * CHUNK, CHUNK)], slope.at[pl.ds(i * CHUNK, CHUNK)])
            for i in range(n // CHUNK)
        ]
        i_copies = load_weight(copies, w_in_ref, w_in, yl)
        f_copies = load_rows(copies, feat_refs, f)
        last = []
        wait(w_copies)
        for i in order:
            wait(r_copies[2 * i : 2 * i + 2])
            wait(s_copies[i : i + 1])
            at = pl.ds(i * CHUNK, CHUNK)
            act_grad = contract(r[at, :], w_out[...], 1, 0)
            pre[at, :] = (act_grad * slope[at, :].astype(F32)).astype(BF)
        wait(i_copies)
        for i in order:
            at = pl.ds(i * CHUNK, CHUNK)
            branch[at, :] = contract(pre[at, :], w_in[...], 1, 1).astype(BF)
            out = own_out if i * CHUNK < half else other_out
            last.append(copies.start(branch.at[at], out.at[pl.ds(i * CHUNK % half, CHUNK)]))
        wait(f_copies)
        for j in range(d // BLOCK):
            at = pl.ds(j * BLOCK, BLOCK)
            grad[at, :] = contract(f[:, j * BLOCK : (j + 1) * BLOCK], pre[...], 0, 0).astype(BF)
            for k in range(BLOCK // 128):
                row = j * BLOCK + k * 128
                to = row // 128 % 4 * 256 + row // 512 * 128
                last.append(
                    copies.start(grad.at[pl.ds(row, 128)], grad_out.at[pl.ds(to, 128)])
                )
        wait(last)

    return kernel_of(
        body,
        [(half, d), (half, d), (d, m)],
        [(n, d), (d, m), (n, m), (d, m), (n, d), (n, m), (n, d), (d, m)],
        48,
        6 * n * d * m,
        place,
        *rows,
        got_out,
        slope,
        got_in,
        *feats,
    )


def columns(shard, place):
    half = shard.shape[1] // 2
    return lax.dynamic_slice_in_dim(shard, place * half, half, 1)


def swap_yl(part):
    return lax.ppermute(part, "yl", [(0, 1), (1, 0)])


def hops(images, ids, blocks, temper, offset, device, waiting):
    rows, width = blocks[0].shape
    count = len(blocks)

    def kernel(*refs):
        image_ref, id_ref = refs[:2]
        block_refs = refs[2 : 2 + count]
        temper_ref, offset_ref, device_ref = refs[2 + count : 5 + count]
        outs = refs[6 + count :]
        local = lax.broadcasted_iota(jnp.int32, (rows, 1), 0)
        for k in range(count):
            logits = temper_ref[0] * contract(block_refs[k][...], image_ref[...], 1, 1)
            logits = logits + offset_ref[0]
            holder = lax.rem(device_ref[0] - k + 128, 128)
            positive = (holder * rows + local == id_ref[...]).astype(F32)
            pair_grad = (jax.nn.sigmoid(logits) - positive).astype(BF)
            outs[count][pl.ds(k * rows, rows), :] = pair_grad
            term = temper_ref[0] * contract(pair_grad, image_ref[...], 1, 0)
            outs[k][...] = term.astype(outs[k].dtype)

    vmem = pl.BlockSpec(memory_space=pltpu.VMEM)
    smem = pl.BlockSpec(memory_space=pltpu.SMEM)
    kinds = [F32] + [BF] * (count - 1)
    return pl.pallas_call(
        kernel,
        out_shape=[jax.ShapeDtypeStruct((rows, width), kind) for kind in kinds]
        + [
            jax.ShapeDtypeStruct((count * rows, images.shape[0]), BF),
            jax.ShapeDtypeStruct(waiting.shape, waiting.dtype),
        ],
        in_specs=[vmem] * (2 + count) + [smem] * 3 + [pl.BlockSpec(memory_space=pl.ANY)],
        out_specs=[vmem] * (count + 1) + [pl.BlockSpec(memory_space=pl.ANY)],
        input_output_aliases={5 + count: count + 1},
        compiler_params=pltpu.CompilerParams(vmem_limit_bytes=16 << 20),
    )(images, ids, *blocks, temper, offset, device, waiting)


def image_side(pair_grad, blocks, temper):
    rows, width = blocks[0].shape
    count = len(blocks)
    n = pair_grad.shape[1]

    def kernel(*refs):
        pair, temper_ref, out = refs[0], refs[1 + count], refs[2 + count]
        total = jnp.zeros((n, width), F32)
        for k in range(count):
            total = total + contract(pair[pl.ds(k * rows, rows), :], refs[1 + k][...], 0, 0)
        out[...] = (temper_ref[0] * total).astype(BF)

    vmem = pl.BlockSpec(memory_space=pltpu.VMEM)
    return pl.pallas_call(
        kernel,
        out_shape=jax.ShapeDtypeStruct((n, width), BF),
        in_specs=[vmem] * (1 + count) + [pl.BlockSpec(memory_space=pltpu.SMEM)],
        out_specs=vmem,
        compiler_params=pltpu.CompilerParams(vmem_limit_bytes=16 << 20),
    )(pair_grad, *blocks, temper)


def add_groups(got, pieces):
    _, n, m = got.shape

    def kernel(parts, out):
        out[...] = parts[0].astype(F32).sum(0).astype(BF)

    return call(
        kernel,
        (pieces,),
        [pl.BlockSpec((1, 4, n, m), lambda j: (j, 0, 0, 0))],
        [(pl.BlockSpec((n, m), lambda j: (0, j)), jax.ShapeDtypeStruct((n, pieces * m), BF))],
        got.reshape(pieces, 4, n, m),
    )[0]


def to_owners(partial):
    return lax.all_to_all(partial, ("yl", "x"), 0, 0, tiled=True).reshape(8, 128, 1024)


def grad_by_x(partial, place):
    got = lax.all_to_all(partial, "x", 0, 0, tiled=True).reshape(4, 2, 128, 1024)
    n, m = got.shape[2:]
    vmem = pl.BlockSpec(memory_space=pltpu.VMEM)
    smem = pl.BlockSpec(memory_space=pltpu.SMEM)
    params = pltpu.CompilerParams(vmem_limit_bytes=20 << 20)

    def add(yl, parts, mine, theirs):
        mine[...] = parts[:, yl[0]].astype(F32).sum(0).astype(BF)
        theirs[...] = parts[:, 1 - yl[0]].astype(F32).sum(0).astype(BF)

    mine, theirs = pl.pallas_call(
        add,
        out_shape=[jax.ShapeDtypeStruct((n, m), BF)] * 2,
        in_specs=[smem, vmem],
        out_specs=[vmem] * 2,
        compiler_params=params,
    )(place, got)

    def join(yl, own, received, out):
        first = yl[0] == 0
        out[:, :m] = jnp.where(first, own[...], received[...])
        out[:, m:] = jnp.where(first, received[...], own[...])

    return pl.pallas_call(
        join,
        out_shape=jax.ShapeDtypeStruct((n, 2 * m), BF),
        in_specs=[smem, vmem, vmem],
        out_specs=vmem,
        compiler_params=params,
    )(place, mine, swap_yl(theirs))


def shards(images, caption_ids, captions, caption_feats, w_in, w_out, logit_scale, logit_bias):
    device = lax.axis_index(AXES).astype(jnp.int32).reshape(1)
    yl = lax.axis_index("yl")
    place = yl.astype(jnp.int32).reshape(1)

    blocks = [captions] + [from_behind(captions, AXES, k) for k in range(1, HOPS + 1)]
    feats_part = gather_first(caption_feats)
    in_parts = [columns(w_in, yl), swap_yl(columns(w_in, 1 - yl))]
    out_parts = [columns(w_out, yl), swap_yl(columns(w_out, 1 - yl))]
    *terms, pair_grad, feats_part = hops(
        images, caption_ids.reshape(1, -1), blocks, logit_scale, logit_bias, device, feats_part
    )
    feats_own, feats_other = gather_second(feats_part)
    parts = [terms[0]] + [from_behind(terms[k], AXES, -k) for k in range(1, HOPS + 1)]
    own_grad, caption_round = add_hops(parts, ())
    got_in = spread(in_parts, (caption_round, out_parts[1]))
    rows_part = gather_first(caption_round, feats_own)
    rows_own, rows_other = gather_second(rows_part)
    got_out = spread(out_parts, rows_own[1:])
    image_grad = image_side(pair_grad, blocks, logit_scale)

    feats = feats_own + feats_other
    rows = rows_own + rows_other
    slope, out_part = forward(place, feats, got_in, rows)
    out_got = to_owners(out_part)
    w_out_grad = add_groups(out_got, 2)
    other, own, in_part = backward(place, rows, got_out, slope, got_in, feats)
    w_in_grad = grad_by_x(behind(in_part, out_got), place)
    feat_grad = scatter_rows(own, other, own_grad)
    return (image_grad, feat_grad, w_in_grad, w_out_grad)


def solution(mesh):
    fine = Mesh(mesh.devices.reshape(2, 4, 2, 4, 2), AXES)
    rows = P(AXES, None)
    weights = P(("yl", "x"), ("yh", "z", "c"))
    return jax.shard_map(
        shards,
        mesh=fine,
        in_specs=(rows, P(AXES), rows, rows, weights, weights, P(), P()),
        out_specs=(rows, rows, weights, weights),
        check_vma=False,
    )
```

```python
import math

import jax
import jax.numpy as jnp
from jax import lax
from jax.experimental import pallas as pl
from jax.experimental.pallas import tpu as pltpu
from jax.sharding import Mesh
from jax.sharding import PartitionSpec as P

HOPS = 2
AXES = ("yl", "x", "yh", "z", "c")
BF = jnp.bfloat16
F32 = jnp.float32


def from_behind(shard, axis, by):
    length = lax.axis_size(axis)
    return lax.ppermute(shard, axis, [(i, (i + by) % length) for i in range(length)])


def step_pairs(first, by):
    pairs = []
    for yl in range(2):
        for yh in range(2):
            for z in range(4):
                for c in range(2):
                    if (c == 0) == first:
                        to = (yl, yh, (z + by) % 4, c)
                    else:
                        y = (yh * 2 + yl + by) % 4
                        to = (y % 2, y // 2, z, c)
                    pairs.append((flat(yl, yh, z, c), flat(*to)))
    return pairs


def flat(yl, yh, z, c):
    return ((yl * 2 + yh) * 4 + z) * 2 + c


def step(shard, first, by):
    return lax.ppermute(shard, ("yl", "yh", "z", "c"), step_pairs(first, by))


def swap_core(shard):
    return lax.ppermute(shard, "c", [(0, 1), (1, 0)])


def pack(pieces):
    rows, width = pieces[0].shape
    count = len(pieces)

    def kernel(*refs):
        out, sem = refs[-2], refs[-1]
        copies = [
            pltpu.make_async_copy(refs[i], out.at[pl.ds(i * rows, rows)], sem.at[i])
            for i in range(count)
        ]
        for copy in copies:
            copy.start()
        for copy in copies:
            copy.wait()

    return pl.pallas_call(
        kernel,
        out_shape=jax.ShapeDtypeStruct((rows * count, width), pieces[0].dtype),
        in_specs=[pl.BlockSpec(memory_space=pl.ANY)] * count,
        out_specs=pl.BlockSpec(memory_space=pltpu.VMEM),
        scratch_shapes=[pltpu.SemaphoreType.DMA((count,))],
        compiler_params=pltpu.CompilerParams(vmem_limit_bytes=16 << 20),
    )(*pieces)


def gelu_parts(values):
    coefficient = math.sqrt(2.0 / math.pi)
    square = values * values
    tangent = jnp.tanh(values * (coefficient + coefficient * 0.044715 * square))
    share = 0.5 + 0.5 * tangent
    output = values * share
    gelu_slope = share + output * (1.0 - share) * (
        2.0 * coefficient + 6.0 * coefficient * 0.044715 * square
    )
    return (output, gelu_slope)


def contract(left_side, right_side, left_dim, right_dim):
    return lax.dot_general(
        left_side,
        right_side,
        (((left_dim,), (right_dim,)), ((), ())),
        preferred_element_type=F32,
    )


def gather_first(block):
    return [block] + [step(block, True, k) for k in range(1, 4)]


def gather_second(block):
    own = [block] + [step(block, False, k) for k in range(1, 4)]
    return own, [swap_core(piece) for piece in own]


def add_split(arrays):
    n, width = arrays[0].shape
    rows = n // 4
    count = len(arrays)

    def kernel(*refs):
        for k in range(4):
            at = pl.ds(k * rows, rows)
            total = refs[0][at, :].astype(F32)
            for a in refs[1:count]:
                total = total + a[at, :].astype(F32)
            refs[count + k][...] = total.astype(refs[count + k].dtype)

    vmem = pl.BlockSpec(memory_space=pltpu.VMEM)
    return pl.pallas_call(
        kernel,
        out_shape=[jax.ShapeDtypeStruct((rows, width), kind) for kind in (F32, BF, BF, BF)],
        in_specs=[vmem] * count,
        out_specs=[vmem] * 4,
        compiler_params=pltpu.CompilerParams(vmem_limit_bytes=20 << 20),
    )(*arrays)


def scatter_rows(parts, own_grad):
    received = [step(parts[k], False, -k) for k in range(1, 4)]
    parts = add_split([parts[0]] + received)
    return add_branch(parts[0], [step(parts[k], True, -k) for k in range(1, 4)], own_grad)


def add_branch(own, received, own_grad):
    rows, width = own.shape

    def kernel(a, b, c, d, grad, out):
        value = a[...] + b[...].astype(F32) + c[...].astype(F32) + d[...].astype(F32)
        out[...] = (grad[...] + value).astype(BF)

    whole = pl.BlockSpec((rows, width), lambda: (0, 0))
    return call(
        kernel,
        (),
        [whole] * 5,
        [(whole, jax.ShapeDtypeStruct((rows, width), BF))],
        own,
        *received,
        own_grad,
    )[0]


def call(kernel, grid, ins, outs, *args, after=(), flops=0):
    taken = len(args)

    def body(*refs):
        kernel(*refs[:taken], *refs[taken + len(after) :])

    return pl.pallas_call(
        body,
        grid=grid,
        in_specs=ins + [pl.BlockSpec(memory_space=pl.ANY)] * len(after),
        out_specs=[spec for spec, _ in outs],
        out_shape=[shape for _, shape in outs],
        compiler_params=pltpu.CompilerParams(vmem_limit_bytes=20 << 20),
        cost_estimate=pl.CostEstimate(
            flops=flops,
            bytes_accessed=sum(a.size * a.dtype.itemsize for a in args)
            + sum(shape.size * shape.dtype.itemsize for _, shape in outs),
            transcendentals=0,
        ),
    )(*args, *after)


def add_hops(parts, after):
    rows, width = parts[0].shape

    def kernel(a, b, c, total, rounded):
        value = a[...] + b[...].astype(F32) + c[...].astype(F32)
        total[...] = value
        rounded[...] = value.astype(BF)

    whole = pl.BlockSpec((rows, width), lambda: (0, 0))
    return call(
        kernel,
        (),
        [whole] * 3,
        [(whole, jax.ShapeDtypeStruct((rows, width), kind)) for kind in (F32, BF)],
        *parts,
        after=after,
    )


def local_copies(plan, out, count, *args, vmem=61):
    def kernel(*refs):
        target, sem = refs[-2], refs[-1]
        copies = [
            pltpu.make_async_copy(a, b, sem.at[i])
            for i, (a, b) in enumerate(plan(refs[:-2], target))
        ]
        for copy in copies:
            copy.start()
        for copy in copies:
            copy.wait()

    return pl.pallas_call(
        kernel,
        out_shape=jax.ShapeDtypeStruct(out, BF),
        in_specs=[
            pl.BlockSpec(memory_space=pltpu.SMEM if a.dtype == jnp.int32 else pl.ANY) for a in args
        ],
        out_specs=pl.BlockSpec(memory_space=pltpu.VMEM),
        scratch_shapes=[pltpu.SemaphoreType.DMA((count,))],
        compiler_params=pltpu.CompilerParams(vmem_limit_bytes=vmem << 20),
    )(*args)


def half_of(shard, yl):
    m = shard.shape[1] // 2
    return shard.at[:, pl.ds(pl.multiple_of(yl * m, m), m)]


def other_columns(place, weights, after):
    n, m = weights[0].shape

    def plan(refs, out):
        other = 1 - refs[0][0]
        return [
            (half_of(refs[1 + w], other), out.at[pl.ds(w * n, n)]) for w in range(len(weights))
        ]

    return local_copies(plan, (len(weights) * n, m // 2), len(weights), place, *weights, *after)


def spread(place, weights, received, after=()):
    n, m = weights[0].shape[0], weights[0].shape[1] // 2
    count = len(weights)

    def kernel(*refs):
        yl = refs[0][0]
        weight_refs, received_ref = refs[1 : 1 + count], refs[1 + count]
        out, held, sem = refs[-3:]
        copies = Copies(sem)
        loads = []
        for w in range(count):
            loads.append(copies.start(half_of(weight_refs[w], yl), held.at[w, 0]))
            loads.append(copies.start(received_ref.at[pl.ds(w * n, n)], held.at[w, 1]))
        wait(loads)
        wait([copies.start(held, out.at[x]) for x in range(4)])

    sent = pl.pallas_call(
        kernel,
        out_shape=jax.ShapeDtypeStruct((4, count, 2, n, m), BF),
        in_specs=[pl.BlockSpec(memory_space=pltpu.SMEM)]
        + [pl.BlockSpec(memory_space=pl.ANY)] * (1 + count + len(after)),
        out_specs=pl.BlockSpec(memory_space=pltpu.HBM),
        scratch_shapes=[
            pltpu.VMEM((count, 2, n, m), BF),
            pltpu.SemaphoreType.DMA((2 * count + 4,)),
        ],
        compiler_params=pltpu.CompilerParams(vmem_limit_bytes=61 << 20),
    )(place, *weights, received, *after)
    return lax.all_to_all(sent, "x", 0, 0, tiled=True)


def kernel_of(body, outs, scratch, copies, flops, place, *arrays):
    vmem = [pltpu.VMEM(shape, BF) for shape in scratch]
    return pl.pallas_call(
        body,
        out_shape=[jax.ShapeDtypeStruct(shape, BF) for shape in outs],
        in_specs=[pl.BlockSpec(memory_space=pltpu.SMEM)]
        + [pl.BlockSpec(memory_space=pl.ANY)] * len(arrays),
        out_specs=[pl.BlockSpec(memory_space=pl.ANY)] * len(outs),
        scratch_shapes=vmem + [pltpu.SemaphoreType.DMA((copies,))],
        compiler_params=pltpu.CompilerParams(vmem_limit_bytes=60 << 20),
        cost_estimate=pl.CostEstimate(
            flops=flops,
            bytes_accessed=2 * sum(a.size for a in arrays) + 2 * sum(math.prod(o) for o in outs),
            transcendentals=0,
        ),
    )(place, *arrays)


class Copies:
    def __init__(self, sem):
        self.sem, self.count = sem, 0

    def start(self, source, target):
        copy = pltpu.make_async_copy(source, target, self.sem.at[self.count])
        self.count += 1
        copy.start()
        return copy


def load_rows(copies, pieces, which, target):
    n = pieces[0].shape[0] // 2
    return [
        copies.start(piece.at[pl.ds(which * n, n)], target.at[pl.ds(i * n, n)])
        for i, piece in enumerate(pieces)
    ]


def load_weight(copies, got, which, target, yl):
    return [
        copies.start(
            got.at[x, which, k],
            target.at[pl.ds(pl.multiple_of(lax.rem(yl + k, 2) * 512 + x * 128, 128), 128)],
        )
        for k in range(2)
        for x in range(4)
    ]


def wait(copies):
    for copy in copies:
        copy.wait()


CHUNK = 512
BLOCK = 256


def forward(place, pieces, got):
    n, d, m = 4 * pieces[0].shape[0], pieces[0].shape[1], got.shape[-1]

    def body(*refs):
        yl = refs[0][0]
        piece_refs, w_ref = refs[1:9], refs[9]
        slope_out, grad_out = refs[10:12]
        f, w, r, active, slope, grad, sem = refs[12:]
        copies = Copies(sem)
        w_copies = load_weight(copies, w_ref, 0, w, yl)
        f_copies = load_rows(copies, piece_refs, 0, f)
        r_copies = load_rows(copies, piece_refs, 1, r)
        last = []
        wait(w_copies)
        for i in range(n // CHUNK):
            wait(f_copies[2 * i : 2 * i + 2])
            at = pl.ds(i * CHUNK, CHUNK)
            output, gelu_slope = gelu_parts(contract(f[at, :], w[...], 1, 0))
            active[at, :] = output.astype(BF)
            slope[at, :] = gelu_slope.astype(BF)
            last.append(copies.start(slope.at[at], slope_out.at[at]))
        wait(r_copies)
        for j in range(d // BLOCK):
            at = pl.ds(j * BLOCK, BLOCK)
            grad[at, :] = contract(r[:, j * BLOCK : (j + 1) * BLOCK], active[...], 0, 0).astype(BF)
            for k in range(BLOCK // 128):
                row = j * BLOCK + k * 128
                to = row // 128 % 4 * 256 + row // 512 * 128
                last.append(
                    copies.start(grad.at[pl.ds(row, 128)], grad_out.at[pl.ds(to, 128)])
                )
        wait(last)

    return kernel_of(
        body,
        [(n, m), (d, m)],
        [(n, d), (d, m), (n, d), (n, m), (n, m), (d, m)],
        36,
        4 * n * d * m,
        place,
        *pieces,
        got,
    )


def backward(place, pieces, got, slope):
    n, d, m = 4 * pieces[0].shape[0], pieces[0].shape[1], got.shape[-1]
    half = n // 2

    def body(*refs):
        yl = refs[0][0]
        piece_refs, w_ref, slope_ref = refs[1:9], refs[9], refs[10]
        other_out, own_out, grad_out = refs[11:14]
        r, w_out, slope, w_in, f, pre, branch, grad, sem = refs[14:]
        copies = Copies(sem)
        order = [2, 3, 0, 1]
        w_copies = load_weight(copies, w_ref, 1, w_out, yl)
        r_copies = load_rows(copies, piece_refs, 1, r)
        s_copies = [
            copies.start(slope_ref.at[pl.ds(i * CHUNK, CHUNK)], slope.at[pl.ds(i * CHUNK, CHUNK)])
            for i in range(n // CHUNK)
        ]
        i_copies = load_weight(copies, w_ref, 0, w_in, yl)
        f_copies = load_rows(copies, piece_refs, 0, f)
        last = []
        wait(w_copies)
        for i in order:
            wait(r_copies[2 * i : 2 * i + 2])
            wait(s_copies[i : i + 1])
            at = pl.ds(i * CHUNK, CHUNK)
            act_grad = contract(r[at, :], w_out[...], 1, 0)
            pre[at, :] = (act_grad * slope[at, :].astype(F32)).astype(BF)
        wait(i_copies)
        for i in order:
            at = pl.ds(i * CHUNK, CHUNK)
            branch[at, :] = contract(pre[at, :], w_in[...], 1, 1).astype(BF)
            out = own_out if i * CHUNK < half else other_out
            last.append(copies.start(branch.at[at], out.at[pl.ds(i * CHUNK % half, CHUNK)]))
        wait(f_copies)
        for j in range(d // BLOCK):
            at = pl.ds(j * BLOCK, BLOCK)
            grad[at, :] = contract(f[:, j * BLOCK : (j + 1) * BLOCK], pre[...], 0, 0).astype(BF)
            for k in range(BLOCK // 128):
                row = j * BLOCK + k * 128
                to = row // 128 % 4 * 256 + row // 512 * 128
                last.append(
                    copies.start(grad.at[pl.ds(row, 128)], grad_out.at[pl.ds(to, 128)])
                )
        wait(last)

    return kernel_of(
        body,
        [(half, d), (half, d), (d, m)],
        [(n, d), (d, m), (n, m), (d, m), (n, d), (n, m), (n, d), (d, m)],
        48,
        6 * n * d * m,
        place,
        *pieces,
        got,
        slope,
    )


def swap_yl(part):
    return lax.ppermute(part, "yl", [(0, 1), (1, 0)])


def hops(images, ids, blocks, temper, offset, device, after):
    rows, width = blocks[0].shape
    count = len(blocks)

    def kernel(*refs):
        image_ref, id_ref = refs[:2]
        block_refs = refs[2 : 2 + count]
        temper_ref, offset_ref, device_ref = refs[2 + count : 5 + count]
        outs = refs[5 + count + len(after) :]
        local = lax.broadcasted_iota(jnp.int32, (rows, 1), 0)
        for k in range(count):
            logits = temper_ref[0] * contract(block_refs[k][...], image_ref[...], 1, 1)
            logits = logits + offset_ref[0]
            holder = lax.rem(device_ref[0] - k + 128, 128)
            positive = (holder * rows + local == id_ref[...]).astype(F32)
            pair_grad = (jax.nn.sigmoid(logits) - positive).astype(BF)
            outs[count][pl.ds(k * rows, rows), :] = pair_grad
            term = temper_ref[0] * contract(pair_grad, image_ref[...], 1, 0)
            outs[k][...] = term.astype(outs[k].dtype)

    vmem = pl.BlockSpec(memory_space=pltpu.VMEM)
    smem = pl.BlockSpec(memory_space=pltpu.SMEM)
    kinds = [F32] + [BF] * (count - 1)
    return pl.pallas_call(
        kernel,
        out_shape=[jax.ShapeDtypeStruct((rows, width), kind) for kind in kinds]
        + [jax.ShapeDtypeStruct((count * rows, images.shape[0]), BF)],
        in_specs=[vmem] * (2 + count)
        + [smem] * 3
        + [pl.BlockSpec(memory_space=pl.ANY)] * len(after),
        out_specs=[vmem] * (count + 1),
        compiler_params=pltpu.CompilerParams(vmem_limit_bytes=16 << 20),
    )(images, ids, *blocks, temper, offset, device, *after)


def image_side(pair_grad, blocks, temper):
    rows, width = blocks[0].shape
    count = len(blocks)
    n = pair_grad.shape[1]

    def kernel(*refs):
        pair, temper_ref, out = refs[0], refs[1 + count], refs[2 + count]
        total = jnp.zeros((n, width), F32)
        for k in range(count):
            total = total + contract(pair[pl.ds(k * rows, rows), :], refs[1 + k][...], 0, 0)
        out[...] = (temper_ref[0] * total).astype(BF)

    vmem = pl.BlockSpec(memory_space=pltpu.VMEM)
    return pl.pallas_call(
        kernel,
        out_shape=jax.ShapeDtypeStruct((n, width), BF),
        in_specs=[vmem] * (1 + count) + [pl.BlockSpec(memory_space=pltpu.SMEM)],
        out_specs=vmem,
        compiler_params=pltpu.CompilerParams(vmem_limit_bytes=16 << 20),
    )(pair_grad, *blocks, temper)


def grad_by_x(got, place):
    got = got.reshape(4, 2, 128, 1024)
    n, m = got.shape[2:]
    vmem = pl.BlockSpec(memory_space=pltpu.VMEM)
    smem = pl.BlockSpec(memory_space=pltpu.SMEM)
    params = pltpu.CompilerParams(vmem_limit_bytes=20 << 20)

    def add(yl, parts, mine, theirs):
        mine[...] = parts[:, yl[0]].astype(F32).sum(0).astype(BF)
        theirs[...] = parts[:, 1 - yl[0]].astype(F32).sum(0).astype(BF)

    mine, theirs = pl.pallas_call(
        add,
        out_shape=[jax.ShapeDtypeStruct((n, m), BF)] * 2,
        in_specs=[smem, vmem],
        out_specs=[vmem] * 2,
        compiler_params=params,
    )(place, got)

    def join(yl, own, received, out):
        first = yl[0] == 0
        out[:, :m] = jnp.where(first, own[...], received[...])
        out[:, m:] = jnp.where(first, received[...], own[...])

    return pl.pallas_call(
        join,
        out_shape=jax.ShapeDtypeStruct((n, 2 * m), BF),
        in_specs=[smem, vmem, vmem],
        out_specs=vmem,
        compiler_params=params,
    )(place, mine, swap_yl(theirs))


def shards(images, caption_ids, captions, caption_feats, w_in, w_out, logit_scale, logit_bias):
    device = lax.axis_index(AXES).astype(jnp.int32).reshape(1)
    yl = lax.axis_index("yl")
    place = yl.astype(jnp.int32).reshape(1)

    blocks = [captions] + [from_behind(captions, AXES, k) for k in range(1, HOPS + 1)]
    feats_first = gather_first(caption_feats)
    received = swap_yl(other_columns(place, (w_in, w_out), ()))
    *terms, pair_grad = hops(
        images,
        caption_ids.reshape(1, -1),
        blocks,
        logit_scale,
        logit_bias,
        device,
        (),
    )
    parts = [terms[0]] + [from_behind(terms[k], AXES, -k) for k in range(1, HOPS + 1)]
    own_grad, caption_round = add_hops(parts, (received, *feats_first[1:]))
    got = spread(place, (w_in, w_out), received, (caption_round,))
    own_rows, other_rows = gather_second(pack(feats_first + gather_first(caption_round)))
    pieces = own_rows + other_rows
    image_grad = image_side(pair_grad, blocks, logit_scale)

    slope, out_part = forward(place, pieces, got)
    out_got = lax.all_to_all(out_part, "x", 0, 0, tiled=True)
    w_out_grad = grad_by_x(out_got, place)
    other, own, in_part = backward(place, pieces, got, slope)
    first = add_split([own, swap_core(other)])
    w_in_grad = grad_by_x(lax.all_to_all(in_part, "x", 0, 0, tiled=True), place)
    feat_grad = scatter_rows(first, own_grad)
    return (image_grad, feat_grad, w_in_grad, w_out_grad)


def solution(mesh):
    fine = Mesh(mesh.devices.reshape(2, 4, 2, 4, 2), AXES)
    rows = P(AXES, None)
    weights = P(("yl", "x"), ("yh", "z", "c"))
    return jax.shard_map(
        shards,
        mesh=fine,
        in_specs=(rows, P(AXES), rows, rows, weights, weights, P(), P()),
        out_specs=(rows, rows, weights, weights),
        check_vma=False,
    )
```

```python
import math

import jax
import jax.numpy as jnp
from jax import lax
from jax.experimental import pallas as pl
from jax.experimental.pallas import tpu as pltpu
from jax.sharding import Mesh
from jax.sharding import PartitionSpec as P

HOPS = 2
AXES = ("yl", "x", "yh", "z", "c")
BF = jnp.bfloat16
F32 = jnp.float32


def from_behind(shard, axis, by):
    length = lax.axis_size(axis)
    return lax.ppermute(shard, axis, [(i, (i + by) % length) for i in range(length)])


def step_pairs(first, by):
    pairs = []
    for yl in range(2):
        for yh in range(2):
            for z in range(4):
                for c in range(2):
                    if (c == 0) == first:
                        to = (yl, yh, (z + by) % 4, c)
                    else:
                        y = (yh * 2 + yl + by) % 4
                        to = (y % 2, y // 2, z, c)
                    pairs.append((flat(yl, yh, z, c), flat(*to)))
    return pairs


def flat(yl, yh, z, c):
    return ((yl * 2 + yh) * 4 + z) * 2 + c


def step(shard, first, by):
    return lax.ppermute(shard, ("yl", "yh", "z", "c"), step_pairs(first, by))


def swap_core(shard):
    return lax.ppermute(shard, "c", [(0, 1), (1, 0)])


def pack(pieces):
    rows, width = pieces[0].shape
    count = len(pieces)

    def kernel(*refs):
        out, sem = refs[-2], refs[-1]
        copies = [
            pltpu.make_async_copy(refs[i], out.at[pl.ds(i * rows, rows)], sem.at[i])
            for i in range(count)
        ]
        for copy in copies:
            copy.start()
        for copy in copies:
            copy.wait()

    return pl.pallas_call(
        kernel,
        out_shape=jax.ShapeDtypeStruct((rows * count, width), pieces[0].dtype),
        in_specs=[pl.BlockSpec(memory_space=pl.ANY)] * count,
        out_specs=pl.BlockSpec(memory_space=pltpu.VMEM),
        scratch_shapes=[pltpu.SemaphoreType.DMA((count,))],
        compiler_params=pltpu.CompilerParams(vmem_limit_bytes=16 << 20),
    )(*pieces)


def gelu_parts(values):
    coefficient = math.sqrt(2.0 / math.pi)
    square = values * values
    tangent = jnp.tanh(values * (coefficient + coefficient * 0.044715 * square))
    share = 0.5 + 0.5 * tangent
    output = values * share
    gelu_slope = share + output * (1.0 - share) * (
        2.0 * coefficient + 6.0 * coefficient * 0.044715 * square
    )
    return (output, gelu_slope)


def contract(left_side, right_side, left_dim, right_dim):
    return lax.dot_general(
        left_side,
        right_side,
        (((left_dim,), (right_dim,)), ((), ())),
        preferred_element_type=F32,
    )


def gather_first(block):
    return [block] + [step(block, True, k) for k in range(1, 4)]


def gather_second(block):
    own = [block] + [step(block, False, k) for k in range(1, 4)]
    return own, [swap_core(piece) for piece in own]


def add_split(arrays):
    n, width = arrays[0].shape
    rows = n // 4
    count = len(arrays)

    def kernel(*refs):
        for k in range(4):
            at = pl.ds(k * rows, rows)
            total = refs[0][at, :].astype(F32)
            for a in refs[1:count]:
                total = total + a[at, :].astype(F32)
            refs[count + k][...] = total.astype(refs[count + k].dtype)

    vmem = pl.BlockSpec(memory_space=pltpu.VMEM)
    return pl.pallas_call(
        kernel,
        out_shape=[jax.ShapeDtypeStruct((rows, width), kind) for kind in (F32, BF, BF, BF)],
        in_specs=[vmem] * count,
        out_specs=[vmem] * 4,
        compiler_params=pltpu.CompilerParams(vmem_limit_bytes=20 << 20),
    )(*arrays)


def scatter_rows(parts, own_grad):
    received = [step(parts[k], False, -k) for k in range(1, 4)]
    parts = add_split([parts[0]] + received)
    return add_branch(parts[0], [step(parts[k], True, -k) for k in range(1, 4)], own_grad)


def add_branch(own, received, own_grad):
    rows, width = own.shape

    def kernel(a, b, c, d, grad, out):
        value = a[...] + b[...].astype(F32) + c[...].astype(F32) + d[...].astype(F32)
        out[...] = (grad[...] + value).astype(BF)

    whole = pl.BlockSpec((rows, width), lambda: (0, 0))
    return call(
        kernel,
        (),
        [whole] * 5,
        [(whole, jax.ShapeDtypeStruct((rows, width), BF))],
        own,
        *received,
        own_grad,
    )[0]


def call(kernel, grid, ins, outs, *args, after=(), flops=0):
    taken = len(args)

    def body(*refs):
        kernel(*refs[:taken], *refs[taken + len(after) :])

    return pl.pallas_call(
        body,
        grid=grid,
        in_specs=ins + [pl.BlockSpec(memory_space=pl.ANY)] * len(after),
        out_specs=[spec for spec, _ in outs],
        out_shape=[shape for _, shape in outs],
        compiler_params=pltpu.CompilerParams(vmem_limit_bytes=20 << 20),
        cost_estimate=pl.CostEstimate(
            flops=flops,
            bytes_accessed=sum(a.size * a.dtype.itemsize for a in args)
            + sum(shape.size * shape.dtype.itemsize for _, shape in outs),
            transcendentals=0,
        ),
    )(*args, *after)


def add_hops(parts, after):
    rows, width = parts[0].shape

    def kernel(a, b, c, total, rounded):
        value = a[...] + b[...].astype(F32) + c[...].astype(F32)
        total[...] = value
        rounded[...] = value.astype(BF)

    whole = pl.BlockSpec((rows, width), lambda: (0, 0))
    return call(
        kernel,
        (),
        [whole] * 3,
        [(whole, jax.ShapeDtypeStruct((rows, width), kind)) for kind in (F32, BF)],
        *parts,
        after=after,
    )


def local_copies(plan, out, count, *args, vmem=61):
    def kernel(*refs):
        target, sem = refs[-2], refs[-1]
        copies = [
            pltpu.make_async_copy(a, b, sem.at[i])
            for i, (a, b) in enumerate(plan(refs[:-2], target))
        ]
        for copy in copies:
            copy.start()
        for copy in copies:
            copy.wait()

    return pl.pallas_call(
        kernel,
        out_shape=jax.ShapeDtypeStruct(out, BF),
        in_specs=[
            pl.BlockSpec(memory_space=pltpu.SMEM if a.dtype == jnp.int32 else pl.ANY) for a in args
        ],
        out_specs=pl.BlockSpec(memory_space=pltpu.VMEM),
        scratch_shapes=[pltpu.SemaphoreType.DMA((count,))],
        compiler_params=pltpu.CompilerParams(vmem_limit_bytes=vmem << 20),
    )(*args)


def half_of(shard, yl):
    m = shard.shape[1] // 2
    return shard.at[:, pl.ds(pl.multiple_of(yl * m, m), m)]


def other_columns(place, weights, after):
    n, m = weights[0].shape

    def plan(refs, out):
        other = 1 - refs[0][0]
        return [
            (half_of(refs[1 + w], other), out.at[pl.ds(w * n, n)]) for w in range(len(weights))
        ]

    return local_copies(plan, (len(weights) * n, m // 2), len(weights), place, *weights, *after)


def spread(place, weights, received):
    n, m = weights[0].shape[0], weights[0].shape[1] // 2
    count = len(weights)

    def kernel(*refs):
        yl = refs[0][0]
        weight_refs, received_ref = refs[1 : 1 + count], refs[1 + count]
        out, token, held, sem = refs[-4:]
        token[...] = jnp.zeros_like(token)
        copies = Copies(sem)
        loads = []
        for w in range(count):
            loads.append(copies.start(half_of(weight_refs[w], yl), held.at[w, 0]))
            loads.append(copies.start(received_ref.at[pl.ds(w * n, n)], held.at[w, 1]))
        wait(loads)
        wait([copies.start(held, out.at[x]) for x in range(4)])

    return pl.pallas_call(
        kernel,
        out_shape=[
            jax.ShapeDtypeStruct((4, count, 2, n, m), BF),
            jax.ShapeDtypeStruct((8, 128), F32),
        ],
        in_specs=[pl.BlockSpec(memory_space=pltpu.SMEM)]
        + [pl.BlockSpec(memory_space=pl.ANY)] * (1 + count),
        out_specs=[
            pl.BlockSpec(memory_space=pltpu.HBM),
            pl.BlockSpec(memory_space=pltpu.VMEM),
        ],
        scratch_shapes=[
            pltpu.VMEM((count, 2, n, m), BF),
            pltpu.SemaphoreType.DMA((2 * count + 4,)),
        ],
        compiler_params=pltpu.CompilerParams(vmem_limit_bytes=61 << 20),
    )(place, *weights, received)


def behind(array, after):
    def kernel(*refs):
        pass

    anywhere = pl.BlockSpec(memory_space=pl.ANY)
    return pl.pallas_call(
        kernel,
        out_shape=jax.ShapeDtypeStruct(array.shape, array.dtype),
        in_specs=[anywhere] * 2,
        out_specs=anywhere,
        input_output_aliases={0: 0},
    )(array, after)


def kernel_of(body, outs, scratch, copies, flops, place, *arrays):
    vmem = [pltpu.VMEM(shape, BF) for shape in scratch]
    return pl.pallas_call(
        body,
        out_shape=[jax.ShapeDtypeStruct(shape, BF) for shape in outs],
        in_specs=[pl.BlockSpec(memory_space=pltpu.SMEM)]
        + [pl.BlockSpec(memory_space=pl.ANY)] * len(arrays),
        out_specs=[pl.BlockSpec(memory_space=pl.ANY)] * len(outs),
        scratch_shapes=vmem + [pltpu.SemaphoreType.DMA((copies,))],
        compiler_params=pltpu.CompilerParams(vmem_limit_bytes=60 << 20),
        cost_estimate=pl.CostEstimate(
            flops=flops,
            bytes_accessed=2 * sum(a.size for a in arrays) + 2 * sum(math.prod(o) for o in outs),
            transcendentals=0,
        ),
    )(place, *arrays)


class Copies:
    def __init__(self, sem):
        self.sem, self.count = sem, 0

    def start(self, source, target):
        copy = pltpu.make_async_copy(source, target, self.sem.at[self.count])
        self.count += 1
        copy.start()
        return copy


def load_rows(copies, pieces, which, target):
    n = pieces[0].shape[0] // 2
    return [
        copies.start(piece.at[pl.ds(which * n, n)], target.at[pl.ds(i * n, n)])
        for i, piece in enumerate(pieces)
    ]


def load_weight(copies, got, which, target, yl):
    return [
        copies.start(
            got.at[x, which, k],
            target.at[pl.ds(pl.multiple_of(lax.rem(yl + k, 2) * 512 + x * 128, 128), 128)],
        )
        for k in range(2)
        for x in range(4)
    ]


def wait(copies):
    for copy in copies:
        copy.wait()


CHUNK = 512
BLOCK = 256


def forward(place, pieces, got):
    n, d, m = 4 * pieces[0].shape[0], pieces[0].shape[1], got.shape[-1]

    def body(*refs):
        yl = refs[0][0]
        piece_refs, w_ref = refs[1:9], refs[9]
        slope_out, grad_out = refs[10:12]
        f, w, r, active, slope, grad, sem = refs[12:]
        copies = Copies(sem)
        w_copies = load_weight(copies, w_ref, 0, w, yl)
        f_copies = load_rows(copies, piece_refs, 0, f)
        r_copies = load_rows(copies, piece_refs, 1, r)
        last = []
        wait(w_copies)
        for i in range(n // CHUNK):
            wait(f_copies[2 * i : 2 * i + 2])
            at = pl.ds(i * CHUNK, CHUNK)
            output, gelu_slope = gelu_parts(contract(f[at, :], w[...], 1, 0))
            active[at, :] = output.astype(BF)
            slope[at, :] = gelu_slope.astype(BF)
            last.append(copies.start(slope.at[at], slope_out.at[at]))
        wait(r_copies)
        for j in range(d // BLOCK):
            at = pl.ds(j * BLOCK, BLOCK)
            grad[at, :] = contract(r[:, j * BLOCK : (j + 1) * BLOCK], active[...], 0, 0).astype(BF)
            for k in range(BLOCK // 128):
                row = j * BLOCK + k * 128
                to = row // 128 % 4 * 256 + row // 512 * 128
                last.append(
                    copies.start(grad.at[pl.ds(row, 128)], grad_out.at[pl.ds(to, 128)])
                )
        wait(last)

    return kernel_of(
        body,
        [(n, m), (d, m)],
        [(n, d), (d, m), (n, d), (n, m), (n, m), (d, m)],
        36,
        4 * n * d * m,
        place,
        *pieces,
        got,
    )


def backward(place, pieces, got, slope):
    n, d, m = 4 * pieces[0].shape[0], pieces[0].shape[1], got.shape[-1]
    half = n // 2

    def body(*refs):
        yl = refs[0][0]
        piece_refs, w_ref, slope_ref = refs[1:9], refs[9], refs[10]
        other_out, own_out, grad_out = refs[11:14]
        r, w_out, slope, w_in, f, pre, branch, grad, sem = refs[14:]
        copies = Copies(sem)
        order = [2, 3, 0, 1]
        w_copies = load_weight(copies, w_ref, 1, w_out, yl)
        r_copies = load_rows(copies, piece_refs, 1, r)
        s_copies = [
            copies.start(slope_ref.at[pl.ds(i * CHUNK, CHUNK)], slope.at[pl.ds(i * CHUNK, CHUNK)])
            for i in range(n // CHUNK)
        ]
        i_copies = load_weight(copies, w_ref, 0, w_in, yl)
        f_copies = load_rows(copies, piece_refs, 0, f)
        last = []
        wait(w_copies)
        for i in order:
            wait(r_copies[2 * i : 2 * i + 2])
            wait(s_copies[i : i + 1])
            at = pl.ds(i * CHUNK, CHUNK)
            act_grad = contract(r[at, :], w_out[...], 1, 0)
            pre[at, :] = (act_grad * slope[at, :].astype(F32)).astype(BF)
        wait(i_copies)
        for i in order:
            at = pl.ds(i * CHUNK, CHUNK)
            branch[at, :] = contract(pre[at, :], w_in[...], 1, 1).astype(BF)
            out = own_out if i * CHUNK < half else other_out
            last.append(copies.start(branch.at[at], out.at[pl.ds(i * CHUNK % half, CHUNK)]))
        wait(f_copies)
        for j in range(d // BLOCK):
            at = pl.ds(j * BLOCK, BLOCK)
            grad[at, :] = contract(f[:, j * BLOCK : (j + 1) * BLOCK], pre[...], 0, 0).astype(BF)
            for k in range(BLOCK // 128):
                row = j * BLOCK + k * 128
                to = row // 128 % 4 * 256 + row // 512 * 128
                last.append(
                    copies.start(grad.at[pl.ds(row, 128)], grad_out.at[pl.ds(to, 128)])
                )
        wait(last)

    return kernel_of(
        body,
        [(half, d), (half, d), (d, m)],
        [(n, d), (d, m), (n, m), (d, m), (n, d), (n, m), (n, d), (d, m)],
        48,
        6 * n * d * m,
        place,
        *pieces,
        got,
        slope,
    )


def swap_yl(part):
    return lax.ppermute(part, "yl", [(0, 1), (1, 0)])


def hops(images, ids, blocks, temper, offset, device, after):
    rows, width = blocks[0].shape
    count = len(blocks)

    def kernel(*refs):
        image_ref, id_ref = refs[:2]
        block_refs = refs[2 : 2 + count]
        temper_ref, offset_ref, device_ref = refs[2 + count : 5 + count]
        outs = refs[5 + count + len(after) :]
        local = lax.broadcasted_iota(jnp.int32, (rows, 1), 0)
        for k in range(count):
            logits = temper_ref[0] * contract(block_refs[k][...], image_ref[...], 1, 1)
            logits = logits + offset_ref[0]
            holder = lax.rem(device_ref[0] - k + 128, 128)
            positive = (holder * rows + local == id_ref[...]).astype(F32)
            pair_grad = (jax.nn.sigmoid(logits) - positive).astype(BF)
            outs[count][pl.ds(k * rows, rows), :] = pair_grad
            term = temper_ref[0] * contract(pair_grad, image_ref[...], 1, 0)
            outs[k][...] = term.astype(outs[k].dtype)

    vmem = pl.BlockSpec(memory_space=pltpu.VMEM)
    smem = pl.BlockSpec(memory_space=pltpu.SMEM)
    kinds = [F32] + [BF] * (count - 1)
    return pl.pallas_call(
        kernel,
        out_shape=[jax.ShapeDtypeStruct((rows, width), kind) for kind in kinds]
        + [jax.ShapeDtypeStruct((count * rows, images.shape[0]), BF)],
        in_specs=[vmem] * (2 + count)
        + [smem] * 3
        + [pl.BlockSpec(memory_space=pl.ANY)] * len(after),
        out_specs=[vmem] * (count + 1),
        compiler_params=pltpu.CompilerParams(vmem_limit_bytes=16 << 20),
    )(images, ids, *blocks, temper, offset, device, *after)


def image_side(pair_grad, blocks, temper):
    rows, width = blocks[0].shape
    count = len(blocks)
    n = pair_grad.shape[1]

    def kernel(*refs):
        pair, temper_ref, out = refs[0], refs[1 + count], refs[2 + count]
        total = jnp.zeros((n, width), F32)
        for k in range(count):
            total = total + contract(pair[pl.ds(k * rows, rows), :], refs[1 + k][...], 0, 0)
        out[...] = (temper_ref[0] * total).astype(BF)

    vmem = pl.BlockSpec(memory_space=pltpu.VMEM)
    return pl.pallas_call(
        kernel,
        out_shape=jax.ShapeDtypeStruct((n, width), BF),
        in_specs=[vmem] * (1 + count) + [pl.BlockSpec(memory_space=pltpu.SMEM)],
        out_specs=vmem,
        compiler_params=pltpu.CompilerParams(vmem_limit_bytes=16 << 20),
    )(pair_grad, *blocks, temper)


def grad_by_x(got, place):
    got = got.reshape(4, 2, 128, 1024)
    n, m = got.shape[2:]
    vmem = pl.BlockSpec(memory_space=pltpu.VMEM)
    smem = pl.BlockSpec(memory_space=pltpu.SMEM)
    params = pltpu.CompilerParams(vmem_limit_bytes=20 << 20)

    def add(yl, parts, out, theirs, mine, sem):
        theirs[...] = parts[:, 1 - yl[0]].astype(F32).sum(0).astype(BF)
        mine[...] = parts[:, yl[0]].astype(F32).sum(0).astype(BF)
        copy = pltpu.make_async_copy(mine, half_of(out, yl[0]), sem)
        copy.start()
        copy.wait()

    anywhere = pl.BlockSpec(memory_space=pl.ANY)
    whole = jax.ShapeDtypeStruct((n, 2 * m), BF)
    grad, theirs = pl.pallas_call(
        add,
        out_shape=[whole, jax.ShapeDtypeStruct((n, m), BF)],
        in_specs=[smem, vmem],
        out_specs=[anywhere, vmem],
        scratch_shapes=[pltpu.VMEM((n, m), BF), pltpu.SemaphoreType.DMA],
        compiler_params=params,
    )(place, got)

    def join(yl, received, given, out, sem):
        copy = pltpu.make_async_copy(received, half_of(out, 1 - yl[0]), sem)
        copy.start()
        copy.wait()

    return pl.pallas_call(
        join,
        out_shape=whole,
        in_specs=[smem, vmem, anywhere],
        out_specs=anywhere,
        input_output_aliases={2: 0},
        scratch_shapes=[pltpu.SemaphoreType.DMA],
        compiler_params=params,
    )(place, swap_yl(theirs), grad)


def shards(images, caption_ids, captions, caption_feats, w_in, w_out, logit_scale, logit_bias):
    device = lax.axis_index(AXES).astype(jnp.int32).reshape(1)
    yl = lax.axis_index("yl")
    place = yl.astype(jnp.int32).reshape(1)

    blocks = [captions] + [from_behind(captions, AXES, k) for k in range(1, HOPS + 1)]
    feats_first = gather_first(caption_feats)
    received = swap_yl(other_columns(place, (w_in, w_out), ()))
    *terms, pair_grad = hops(
        images,
        caption_ids.reshape(1, -1),
        blocks,
        logit_scale,
        logit_bias,
        device,
        (),
    )
    sent, token = spread(place, (w_in, w_out), received)
    parts = [terms[0]] + [from_behind(terms[k], AXES, -k) for k in range(1, HOPS + 1)]
    own_grad, caption_round = add_hops(parts, (token, *feats_first[1:]))
    got = lax.all_to_all(behind(sent, caption_round), "x", 0, 0, tiled=True)
    own_rows, other_rows = gather_second(pack(feats_first + gather_first(caption_round)))
    pieces = own_rows + other_rows
    image_grad = image_side(pair_grad, blocks, logit_scale)

    slope, out_part = forward(place, pieces, got)
    out_got = lax.all_to_all(out_part, "x", 0, 0, tiled=True)
    w_out_grad = grad_by_x(out_got, place)
    other, own, in_part = backward(place, pieces, got, slope)
    first = add_split([own, swap_core(other)])
    w_in_grad = grad_by_x(lax.all_to_all(in_part, "x", 0, 0, tiled=True), place)
    feat_grad = scatter_rows(first, own_grad)
    return (image_grad, feat_grad, w_in_grad, w_out_grad)


def solution(mesh):
    fine = Mesh(mesh.devices.reshape(2, 4, 2, 4, 2), AXES)
    rows = P(AXES, None)
    weights = P(("yl", "x"), ("yh", "z", "c"))
    return jax.shard_map(
        shards,
        mesh=fine,
        in_specs=(rows, P(AXES), rows, rows, weights, weights, P(), P()),
        out_specs=(rows, rows, weights, weights),
        check_vma=False,
    )
```

```python
import math

import jax
import jax.numpy as jnp
from jax import lax
from jax.experimental import pallas as pl
from jax.experimental.pallas import tpu as pltpu
from jax.sharding import Mesh
from jax.sharding import PartitionSpec as P

HOPS = 2
AXES = ("yl", "x", "yh", "z", "c")
BF = jnp.bfloat16
F32 = jnp.float32


def from_behind(shard, axis, by):
    length = lax.axis_size(axis)
    return lax.ppermute(shard, axis, [(i, (i + by) % length) for i in range(length)])


def step_pairs(first, by):
    pairs = []
    for yl in range(2):
        for yh in range(2):
            for z in range(4):
                for c in range(2):
                    if (c == 0) == first:
                        to = (yl, yh, (z + by) % 4, c)
                    else:
                        y = (yh * 2 + yl + by) % 4
                        to = (y % 2, y // 2, z, c)
                    pairs.append((flat(yl, yh, z, c), flat(*to)))
    return pairs


def flat(yl, yh, z, c):
    return ((yl * 2 + yh) * 4 + z) * 2 + c


def step(shard, first, by):
    return lax.ppermute(shard, ("yl", "yh", "z", "c"), step_pairs(first, by))


def swap_core(shard):
    return lax.ppermute(shard, "c", [(0, 1), (1, 0)])


def pack(pieces):
    rows, width = pieces[0].shape
    count = len(pieces)

    def kernel(*refs):
        out, sem = refs[-2], refs[-1]
        copies = [
            pltpu.make_async_copy(refs[i], out.at[pl.ds(i * rows, rows)], sem.at[i])
            for i in range(count)
        ]
        for copy in copies:
            copy.start()
        for copy in copies:
            copy.wait()

    return pl.pallas_call(
        kernel,
        out_shape=jax.ShapeDtypeStruct((rows * count, width), pieces[0].dtype),
        in_specs=[pl.BlockSpec(memory_space=pl.ANY)] * count,
        out_specs=pl.BlockSpec(memory_space=pltpu.VMEM),
        scratch_shapes=[pltpu.SemaphoreType.DMA((count,))],
        compiler_params=pltpu.CompilerParams(vmem_limit_bytes=16 << 20),
    )(*pieces)


def gelu_parts(values):
    coefficient = math.sqrt(2.0 / math.pi)
    square = values * values
    tangent = jnp.tanh(values * (coefficient + coefficient * 0.044715 * square))
    share = 0.5 + 0.5 * tangent
    output = values * share
    gelu_slope = share + output * (1.0 - share) * (
        2.0 * coefficient + 6.0 * coefficient * 0.044715 * square
    )
    return (output, gelu_slope)


def contract(left_side, right_side, left_dim, right_dim):
    return lax.dot_general(
        left_side,
        right_side,
        (((left_dim,), (right_dim,)), ((), ())),
        preferred_element_type=F32,
    )


def gather_first(block):
    return [block] + [step(block, True, k) for k in range(1, 4)]


def gather_second(block):
    own = [block] + [step(block, False, k) for k in range(1, 4)]
    return own, [swap_core(piece) for piece in own]


def add_split(arrays):
    n, width = arrays[0].shape
    rows = n // 4
    count = len(arrays)

    def kernel(*refs):
        for k in range(4):
            at = pl.ds(k * rows, rows)
            total = refs[0][at, :].astype(F32)
            for a in refs[1:count]:
                total = total + a[at, :].astype(F32)
            refs[count + k][...] = total.astype(refs[count + k].dtype)

    vmem = pl.BlockSpec(memory_space=pltpu.VMEM)
    return pl.pallas_call(
        kernel,
        out_shape=[jax.ShapeDtypeStruct((rows, width), kind) for kind in (F32, BF, BF, BF)],
        in_specs=[vmem] * count,
        out_specs=[vmem] * 4,
        compiler_params=pltpu.CompilerParams(vmem_limit_bytes=20 << 20),
    )(*arrays)


def scatter_rows(parts, own_grad):
    received = [step(parts[k], False, -k) for k in range(1, 4)]
    parts = add_split([parts[0]] + received)
    return add_branch(parts[0], [step(parts[k], True, -k) for k in range(1, 4)], own_grad)


def add_branch(own, received, own_grad):
    rows, width = own.shape

    def kernel(a, b, c, d, grad, out):
        value = a[...] + b[...].astype(F32) + c[...].astype(F32) + d[...].astype(F32)
        out[...] = (grad[...] + value).astype(BF)

    whole = pl.BlockSpec((rows, width), lambda: (0, 0))
    return call(
        kernel,
        (),
        [whole] * 5,
        [(whole, jax.ShapeDtypeStruct((rows, width), BF))],
        own,
        *received,
        own_grad,
    )[0]


def call(kernel, grid, ins, outs, *args, after=(), flops=0):
    taken = len(args)

    def body(*refs):
        kernel(*refs[:taken], *refs[taken + len(after) :])

    return pl.pallas_call(
        body,
        grid=grid,
        in_specs=ins + [pl.BlockSpec(memory_space=pl.ANY)] * len(after),
        out_specs=[spec for spec, _ in outs],
        out_shape=[shape for _, shape in outs],
        compiler_params=pltpu.CompilerParams(vmem_limit_bytes=20 << 20),
        cost_estimate=pl.CostEstimate(
            flops=flops,
            bytes_accessed=sum(a.size * a.dtype.itemsize for a in args)
            + sum(shape.size * shape.dtype.itemsize for _, shape in outs),
            transcendentals=0,
        ),
    )(*args, *after)


def add_hops(parts, after):
    rows, width = parts[0].shape

    def kernel(a, b, c, total, rounded):
        value = a[...] + b[...].astype(F32) + c[...].astype(F32)
        total[...] = value
        rounded[...] = value.astype(BF)

    whole = pl.BlockSpec((rows, width), lambda: (0, 0))
    return call(
        kernel,
        (),
        [whole] * 3,
        [(whole, jax.ShapeDtypeStruct((rows, width), kind)) for kind in (F32, BF)],
        *parts,
        after=after,
    )


def local_copies(plan, out, count, *args, vmem=61):
    def kernel(*refs):
        target, sem = refs[-2], refs[-1]
        copies = [
            pltpu.make_async_copy(a, b, sem.at[i])
            for i, (a, b) in enumerate(plan(refs[:-2], target))
        ]
        for copy in copies:
            copy.start()
        for copy in copies:
            copy.wait()

    return pl.pallas_call(
        kernel,
        out_shape=jax.ShapeDtypeStruct(out, BF),
        in_specs=[
            pl.BlockSpec(memory_space=pltpu.SMEM if a.dtype == jnp.int32 else pl.ANY) for a in args
        ],
        out_specs=pl.BlockSpec(memory_space=pltpu.VMEM),
        scratch_shapes=[pltpu.SemaphoreType.DMA((count,))],
        compiler_params=pltpu.CompilerParams(vmem_limit_bytes=vmem << 20),
    )(*args)


def half_of(shard, yl):
    m = shard.shape[1] // 2
    return shard.at[:, pl.ds(pl.multiple_of(yl * m, m), m)]


def other_columns(place, weights, after):
    n, m = weights[0].shape

    def plan(refs, out):
        other = 1 - refs[0][0]
        return [
            (half_of(refs[1 + w], other), out.at[pl.ds(w * n, n)]) for w in range(len(weights))
        ]

    return local_copies(plan, (len(weights) * n, m // 2), len(weights), place, *weights, *after)


def spread(place, weights, received):
    n, m = weights[0].shape[0], weights[0].shape[1] // 2
    count = len(weights)

    def kernel(*refs):
        yl = refs[0][0]
        weight_refs, received_ref = refs[1 : 1 + count], refs[1 + count]
        out, token, held, sem = refs[-4:]
        token[...] = jnp.zeros_like(token)
        copies = Copies(sem)
        loads = []
        for w in range(count):
            loads.append(copies.start(half_of(weight_refs[w], yl), held.at[w, 0]))
            loads.append(copies.start(received_ref.at[pl.ds(w * n, n)], held.at[w, 1]))
        wait(loads)
        wait([copies.start(held, out.at[x]) for x in range(4)])

    return pl.pallas_call(
        kernel,
        out_shape=[
            jax.ShapeDtypeStruct((4, count, 2, n, m), BF),
            jax.ShapeDtypeStruct((8, 128), F32),
        ],
        in_specs=[pl.BlockSpec(memory_space=pltpu.SMEM)]
        + [pl.BlockSpec(memory_space=pl.ANY)] * (1 + count),
        out_specs=[
            pl.BlockSpec(memory_space=pltpu.HBM),
            pl.BlockSpec(memory_space=pltpu.VMEM),
        ],
        scratch_shapes=[
            pltpu.VMEM((count, 2, n, m), BF),
            pltpu.SemaphoreType.DMA((2 * count + 4,)),
        ],
        compiler_params=pltpu.CompilerParams(vmem_limit_bytes=61 << 20),
    )(place, *weights, received)


def behind(array, after):
    def kernel(*refs):
        pass

    anywhere = pl.BlockSpec(memory_space=pl.ANY)
    return pl.pallas_call(
        kernel,
        out_shape=jax.ShapeDtypeStruct(array.shape, array.dtype),
        in_specs=[anywhere] * 2,
        out_specs=anywhere,
        input_output_aliases={0: 0},
    )(array, after)


def kernel_of(body, outs, scratch, copies, flops, place, *arrays):
    vmem = [pltpu.VMEM(shape, BF) for shape in scratch]
    return pl.pallas_call(
        body,
        out_shape=[jax.ShapeDtypeStruct(shape, BF) for shape in outs],
        in_specs=[pl.BlockSpec(memory_space=pltpu.SMEM)]
        + [pl.BlockSpec(memory_space=pl.ANY)] * len(arrays),
        out_specs=[pl.BlockSpec(memory_space=pl.ANY)] * len(outs),
        scratch_shapes=vmem + [pltpu.SemaphoreType.DMA((copies,))],
        compiler_params=pltpu.CompilerParams(vmem_limit_bytes=60 << 20),
        cost_estimate=pl.CostEstimate(
            flops=flops,
            bytes_accessed=2 * sum(a.size for a in arrays) + 2 * sum(math.prod(o) for o in outs),
            transcendentals=0,
        ),
    )(place, *arrays)


class Copies:
    def __init__(self, sem):
        self.sem, self.count = sem, 0

    def start(self, source, target):
        copy = pltpu.make_async_copy(source, target, self.sem.at[self.count])
        self.count += 1
        copy.start()
        return copy


def load_rows(copies, pieces, which, target):
    n = pieces[0].shape[0] // 2
    return [
        copies.start(piece.at[pl.ds(which * n, n)], target.at[pl.ds(i * n, n)])
        for i, piece in enumerate(pieces)
    ]


def load_weight(copies, got, which, target, yl):
    return [
        copies.start(
            got.at[x, which, k],
            target.at[pl.ds(pl.multiple_of(lax.rem(yl + k, 2) * 512 + x * 128, 128), 128)],
        )
        for k in range(2)
        for x in range(4)
    ]


def wait(copies):
    for copy in copies:
        copy.wait()


CHUNK = 512
BLOCK = 256


def forward(place, pieces, got):
    n, d, m = 4 * pieces[0].shape[0], pieces[0].shape[1], got.shape[-1]

    def body(*refs):
        yl = refs[0][0]
        piece_refs, w_ref = refs[1:9], refs[9]
        slope_out, grad_out = refs[10:12]
        f, w, r, active, slope, grad, sem = refs[12:]
        copies = Copies(sem)
        w_copies = load_weight(copies, w_ref, 0, w, yl)
        f_copies = load_rows(copies, piece_refs, 0, f)
        r_copies = load_rows(copies, piece_refs, 1, r)
        last = []
        wait(w_copies)
        for i in range(n // CHUNK):
            wait(f_copies[2 * i : 2 * i + 2])
            at = pl.ds(i * CHUNK, CHUNK)
            output, gelu_slope = gelu_parts(contract(f[at, :], w[...], 1, 0))
            active[at, :] = output.astype(BF)
            slope[at, :] = gelu_slope.astype(BF)
            last.append(copies.start(slope.at[at], slope_out.at[at]))
        wait(r_copies)
        for j in range(d // BLOCK):
            at = pl.ds(j * BLOCK, BLOCK)
            grad[at, :] = contract(r[:, j * BLOCK : (j + 1) * BLOCK], active[...], 0, 0).astype(BF)
            for k in range(BLOCK // 128):
                row = j * BLOCK + k * 128
                to = row // 128 % 4 * 256 + row // 512 * 128
                last.append(
                    copies.start(grad.at[pl.ds(row, 128)], grad_out.at[pl.ds(to, 128)])
                )
        wait(last)

    return kernel_of(
        body,
        [(n, m), (d, m)],
        [(n, d), (d, m), (n, d), (n, m), (n, m), (d, m)],
        36,
        4 * n * d * m,
        place,
        *pieces,
        got,
    )


def backward(place, pieces, got, slope):
    n, d, m = 4 * pieces[0].shape[0], pieces[0].shape[1], got.shape[-1]
    half = n // 2

    def body(*refs):
        yl = refs[0][0]
        piece_refs, w_ref, slope_ref = refs[1:9], refs[9], refs[10]
        other_out, own_out, grad_out = refs[11:14]
        r, w_out, slope, w_in, f, pre, branch, grad, sem = refs[14:]
        copies = Copies(sem)
        order = [2, 3, 0, 1]
        w_copies = load_weight(copies, w_ref, 1, w_out, yl)
        r_copies = load_rows(copies, piece_refs, 1, r)
        s_copies = [
            copies.start(slope_ref.at[pl.ds(i * CHUNK, CHUNK)], slope.at[pl.ds(i * CHUNK, CHUNK)])
            for i in range(n // CHUNK)
        ]
        i_copies = load_weight(copies, w_ref, 0, w_in, yl)
        f_copies = load_rows(copies, piece_refs, 0, f)
        last = []
        wait(w_copies)
        for i in order:
            wait(r_copies[2 * i : 2 * i + 2])
            wait(s_copies[i : i + 1])
            at = pl.ds(i * CHUNK, CHUNK)
            act_grad = contract(r[at, :], w_out[...], 1, 0)
            pre[at, :] = (act_grad * slope[at, :].astype(F32)).astype(BF)
        wait(i_copies)
        for i in order:
            at = pl.ds(i * CHUNK, CHUNK)
            branch[at, :] = contract(pre[at, :], w_in[...], 1, 1).astype(BF)
            out = own_out if i * CHUNK < half else other_out
            last.append(copies.start(branch.at[at], out.at[pl.ds(i * CHUNK % half, CHUNK)]))
        wait(f_copies)
        for j in range(d // BLOCK):
            at = pl.ds(j * BLOCK, BLOCK)
            grad[at, :] = contract(f[:, j * BLOCK : (j + 1) * BLOCK], pre[...], 0, 0).astype(BF)
            for k in range(BLOCK // 128):
                row = j * BLOCK + k * 128
                to = row // 128 % 4 * 256 + row // 512 * 128
                last.append(
                    copies.start(grad.at[pl.ds(row, 128)], grad_out.at[pl.ds(to, 128)])
                )
        wait(last)

    return kernel_of(
        body,
        [(half, d), (half, d), (d, m)],
        [(n, d), (d, m), (n, m), (d, m), (n, d), (n, m), (n, d), (d, m)],
        48,
        6 * n * d * m,
        place,
        *pieces,
        got,
        slope,
    )


def swap_yl(part):
    return lax.ppermute(part, "yl", [(0, 1), (1, 0)])


def hops(images, ids, blocks, temper, offset, device, after):
    rows, width = blocks[0].shape
    count = len(blocks)

    def kernel(*refs):
        image_ref, id_ref = refs[:2]
        block_refs = refs[2 : 2 + count]
        temper_ref, offset_ref, device_ref = refs[2 + count : 5 + count]
        outs = refs[5 + count + len(after) :]
        local = lax.broadcasted_iota(jnp.int32, (rows, 1), 0)
        for k in range(count):
            logits = temper_ref[0] * contract(block_refs[k][...], image_ref[...], 1, 1)
            logits = logits + offset_ref[0]
            holder = lax.rem(device_ref[0] - k + 128, 128)
            positive = (holder * rows + local == id_ref[...]).astype(F32)
            pair_grad = (jax.nn.sigmoid(logits) - positive).astype(BF)
            outs[count][pl.ds(k * rows, rows), :] = pair_grad
            term = temper_ref[0] * contract(pair_grad, image_ref[...], 1, 0)
            outs[k][...] = term.astype(outs[k].dtype)

    vmem = pl.BlockSpec(memory_space=pltpu.VMEM)
    smem = pl.BlockSpec(memory_space=pltpu.SMEM)
    kinds = [F32] + [BF] * (count - 1)
    return pl.pallas_call(
        kernel,
        out_shape=[jax.ShapeDtypeStruct((rows, width), kind) for kind in kinds]
        + [jax.ShapeDtypeStruct((count * rows, images.shape[0]), BF)],
        in_specs=[vmem] * (2 + count)
        + [smem] * 3
        + [pl.BlockSpec(memory_space=pl.ANY)] * len(after),
        out_specs=[vmem] * (count + 1),
        compiler_params=pltpu.CompilerParams(vmem_limit_bytes=16 << 20),
    )(images, ids, *blocks, temper, offset, device, *after)


def image_side(pair_grad, blocks, temper):
    rows, width = blocks[0].shape
    count = len(blocks)
    n = pair_grad.shape[1]

    def kernel(*refs):
        pair, temper_ref, out = refs[0], refs[1 + count], refs[2 + count]
        total = jnp.zeros((n, width), F32)
        for k in range(count):
            total = total + contract(pair[pl.ds(k * rows, rows), :], refs[1 + k][...], 0, 0)
        out[...] = (temper_ref[0] * total).astype(BF)

    vmem = pl.BlockSpec(memory_space=pltpu.VMEM)
    return pl.pallas_call(
        kernel,
        out_shape=jax.ShapeDtypeStruct((n, width), BF),
        in_specs=[vmem] * (1 + count) + [pl.BlockSpec(memory_space=pltpu.SMEM)],
        out_specs=vmem,
        compiler_params=pltpu.CompilerParams(vmem_limit_bytes=16 << 20),
    )(pair_grad, *blocks, temper)


def grad_by_x(got, place):
    got = got.reshape(4, 2, 128, 1024)
    n, m = got.shape[2:]
    vmem = pl.BlockSpec(memory_space=pltpu.VMEM)
    smem = pl.BlockSpec(memory_space=pltpu.SMEM)
    params = pltpu.CompilerParams(vmem_limit_bytes=20 << 20)

    def theirs(yl, parts, out, held, sem):
        copy = pltpu.make_async_copy(parts.at[:, 1 - yl[0]], held, sem)
        copy.start()
        copy.wait()
        out[...] = held[...].astype(F32).sum(0).astype(BF)

    def mine(yl, parts, out, held, total, sem):
        load = pltpu.make_async_copy(parts.at[:, yl[0]], held, sem)
        load.start()
        load.wait()
        total[...] = held[...].astype(F32).sum(0).astype(BF)
        copy = pltpu.make_async_copy(total, half_of(out, yl[0]), sem)
        copy.start()
        copy.wait()

    anywhere = pl.BlockSpec(memory_space=pl.ANY)
    part = jax.ShapeDtypeStruct((n, m), BF)
    whole = jax.ShapeDtypeStruct((n, 2 * m), BF)
    held = pltpu.VMEM((4, n, m), BF)
    swapped = swap_yl(
        pl.pallas_call(
            theirs,
            out_shape=part,
            in_specs=[smem, anywhere],
            out_specs=vmem,
            scratch_shapes=[held, pltpu.SemaphoreType.DMA],
            compiler_params=params,
        )(place, got)
    )
    grad = pl.pallas_call(
        mine,
        out_shape=whole,
        in_specs=[smem, anywhere],
        out_specs=anywhere,
        scratch_shapes=[held, pltpu.VMEM((n, m), BF), pltpu.SemaphoreType.DMA],
        compiler_params=params,
    )(place, got)

    def join(yl, received, given, out, sem):
        copy = pltpu.make_async_copy(received, half_of(out, 1 - yl[0]), sem)
        copy.start()
        copy.wait()

    return pl.pallas_call(
        join,
        out_shape=whole,
        in_specs=[smem, vmem, anywhere],
        out_specs=anywhere,
        input_output_aliases={2: 0},
        scratch_shapes=[pltpu.SemaphoreType.DMA],
        compiler_params=params,
    )(place, swapped, grad)


def shards(images, caption_ids, captions, caption_feats, w_in, w_out, logit_scale, logit_bias):
    device = lax.axis_index(AXES).astype(jnp.int32).reshape(1)
    yl = lax.axis_index("yl")
    place = yl.astype(jnp.int32).reshape(1)

    blocks = [captions] + [from_behind(captions, AXES, k) for k in range(1, HOPS + 1)]
    feats_first = gather_first(caption_feats)
    received = swap_yl(other_columns(place, (w_in, w_out), ()))
    *terms, pair_grad = hops(
        images,
        caption_ids.reshape(1, -1),
        blocks,
        logit_scale,
        logit_bias,
        device,
        (),
    )
    sent, token = spread(place, (w_in, w_out), received)
    parts = [terms[0]] + [from_behind(terms[k], AXES, -k) for k in range(1, HOPS + 1)]
    own_grad, caption_round = add_hops(parts, (token, *feats_first[1:]))
    got = lax.all_to_all(behind(sent, caption_round), "x", 0, 0, tiled=True)
    own_rows, other_rows = gather_second(pack(feats_first + gather_first(caption_round)))
    pieces = own_rows + other_rows
    image_grad = image_side(pair_grad, blocks, logit_scale)

    slope, out_part = forward(place, pieces, got)
    out_got = lax.all_to_all(out_part, "x", 0, 0, tiled=True)
    w_out_grad = grad_by_x(out_got, place)
    other, own, in_part = backward(place, pieces, got, slope)
    first = add_split([own, swap_core(other)])
    w_in_grad = grad_by_x(lax.all_to_all(in_part, "x", 0, 0, tiled=True), place)
    feat_grad = scatter_rows(first, own_grad)
    return (image_grad, feat_grad, w_in_grad, w_out_grad)


def solution(mesh):
    fine = Mesh(mesh.devices.reshape(2, 4, 2, 4, 2), AXES)
    rows = P(AXES, None)
    weights = P(("yl", "x"), ("yh", "z", "c"))
    return jax.shard_map(
        shards,
        mesh=fine,
        in_specs=(rows, P(AXES), rows, rows, weights, weights, P(), P()),
        out_specs=(rows, rows, weights, weights),
        check_vma=False,
    )
```
